512 devices in a mesh: wide: 64 (over y, x, core), narrow: 8 (over z).
Axes of the slice: x: 4, y: 8, z: 8, core: 2. Of those that a mesh axis runs over, the one named last changes fastest.
Arguments:
- tokens: bfloat16 [256, 8192], P('wide', 'narrow'), may hold values from -6 to 6
- cotangent: bfloat16 [256, 8192], P('wide', 'narrow'), may hold values from -4 to 4
- rewards: float32 [256], P('wide'), may hold values from -6 to 6
- group_ids: int32 [256], P('wide'), may hold values from 0 to 15, never falling along the last dimension, each value on 1 to 32 neighbouring positions
- token_mask: int32 [256], P('wide'), may hold values 0 or 1
- w_gate: bfloat16 [8192, 32768], P('narrow', 'wide'), may hold values from -0.0625 to 0.0625
- w_up: bfloat16 [8192, 32768], P('narrow', 'wide'), may hold values from -0.0625 to 0.0625
- down_weight_frozen: bfloat16 [32768, 8192], P('wide', 'narrow'), may hold values from -0.03125 to 0.03125
- a_gate: bfloat16 [8192, 64], P('narrow'), may hold values from -0.0625 to 0.0625
- a_up: bfloat16 [8192, 64], P('narrow'), may hold values from -0.0625 to 0.0625
- gate_output_factor: bfloat16 [64, 32768], P(None, 'wide'), may hold values from -0.375 to 0.375
- up_output_factor: bfloat16 [64, 32768], P(None, 'wide'), may hold values from -0.375 to 0.375
- a_down: bfloat16 [32768, 64], P('wide'), may hold values from -0.03125 to 0.03125
- down_output_factor: bfloat16 [64, 8192], P(None, 'narrow'), may hold values from -0.375 to 0.375
Outputs:
- grad_x: bfloat16 [256, 8192], P('wide', 'narrow')
- divergence: float32 [256], P('wide')
- grad_a_gate: float32 [8192, 64], P('narrow')
- grad_a_up: float32 [8192, 64], P('narrow')
- gate_output_gradient: float32 [64, 32768], P(None, 'wide')
- up_output_gradient: float32 [64, 32768], P(None, 'wide')
- grad_a_down: float32 [32768, 64], P('wide')
- down_output_gradient: float32 [64, 8192], P(None, 'narrow')
The draws below stay inside these ranges and needn't reach their ends.
Inputs may be any that keep to these rules, and one draw needn't show every extreme that they name: `group_ids`: group ids never fall along the tokens; each group holds 1 to 32 tokens.
All inputs are finite; a program needn't handle non-finite values. No bound on the sum of `token_mask` on one device may be relied on, other than what follows from the above.
Results may differ from the reference program's by a relative error of at most 0.035.
Values may be sent and summed in bfloat16 or wider, within the bound.
A program may use at most 64 MiB of HBM per device.

```python
import math
import jax
import jax.numpy as jnp
import numpy as np
from jax import lax

D = 8192
FF = 32768
R = 64
TOKENS = 256
GROUPS = 16
GMAX = 32


def with_ends(values, rng, least, high):
    longest = values.shape.index(max(values.shape))
    spots = []
    for shift in (0, 1):
        where = [jax.random.randint(jax.random.fold_in(rng, axis), (), 0, length) for axis, length in enumerate(values.shape)]
        where[longest] = (where[longest] + shift) % values.shape[longest]
        spots.append(tuple(where))
    return values.at[spots[0]].set(least).at[spots[1]].set(high)


def level_of(rng, shape, shards, smallest, high):
    factor_of, own = 1.0, jax.random.fold_in(rng, 6)
    for axis_at, parts in shards:
        steps = jnp.exp(jax.random.uniform(jax.random.fold_in(own, axis_at), (parts,), jnp.float32, smallest / len(shards), high / len(shards)))
        factor_of = factor_of * jnp.repeat(steps, shape[axis_at] // parts).reshape([-1 if axis == axis_at else 1 for axis in range(len(shape))])
    return factor_of


def split_up(amount, total, reach, lean):
    portions = [(1 << 20) // math.isqrt(standing ** lean) + 1 for standing in range(2, amount + 1)]
    surplus, given = total - reach - (amount - 1), [1] * (amount - 1)
    while surplus > 0:
        free = [i for i in range(amount - 1) if given[i] < reach]
        whole, left = sum([portions[i] for i in free]), surplus
        for i in free:
            addition = min(reach - given[i], max(1, left * portions[i] // whole), surplus)
            given[i] = given[i] + addition
            surplus = surplus - addition
    return np.array([reach] + given)


def ragged(rng, count, total, bound, lean):
    if count == 2:
        one = jax.random.randint(rng, (), max(1, total - bound), min(bound, total - 1) + 1)
        return jnp.stack([one, total - one])
    sizes = jnp.asarray(split_up(count, total, bound, lean), jnp.int32)
    pairs = (count - 1) // 2
    source_of, receiver = sizes[1:1 + 2 * pairs:2], sizes[2:2 + 2 * pairs:2]
    margin = jnp.minimum(source_of - 1, bound - receiver)
    shifted = jax.random.randint(jax.random.fold_in(rng, 1), (pairs,), 0, 1 << 20) % (margin + 1)
    sizes = sizes.at[1:1 + 2 * pairs:2].set(source_of - shifted).at[2:2 + 2 * pairs:2].set(receiver + shifted)
    return sizes[jax.random.permutation(jax.random.fold_in(rng, 2), count)]


def noise(own_key, shape, scale, most, cuts=(), kind=jnp.bfloat16):
    result = jax.random.normal(own_key, shape, jnp.float32) * scale
    if len(cuts) > 0:
        result = level_of(own_key, shape, cuts, -0.22, 0.18) * result
    return jnp.clip(result, min=-most, max=most).astype(kind)


def setup_inputs(seed: int = 0) -> dict:
    arg_keys = jax.random.split(jax.random.key(seed), 15)
    tokens = noise(arg_keys[0], (TOKENS, D), 1.0, 6.0, ((0, 64), (1, 8)))
    cotangent = noise(arg_keys[1], (TOKENS, D), 0.3, 4.0, ((0, 64), (1, 8)))
    rewards = noise(arg_keys[2], (TOKENS,), 1.0, 6.0, ((0, 64),), jnp.float32)
    group_ids = jnp.searchsorted(jnp.cumsum(ragged(arg_keys[3], GROUPS, TOKENS, GMAX, 2)), jnp.arange(TOKENS), side="right").astype(jnp.int32)
    token_mask = with_ends((jax.random.randint(arg_keys[4], (TOKENS,), 0, 4) < 3).astype(jnp.int32), jax.random.fold_in(arg_keys[4], 1), 0, 1)
    w_gate = noise(arg_keys[5], (D, FF), D ** -0.5, 0.0625, ((0, 8), (1, 64)))
    w_up = noise(arg_keys[6], (D, FF), D ** -0.5, 0.0625, ((0, 8), (1, 64)))
    down_weight_frozen = noise(arg_keys[7], (FF, D), FF ** -0.5, 0.03125, ((0, 64), (1, 8)))
    a_gate = noise(arg_keys[8], (D, R), D ** -0.5, 0.0625, ((0, 8),))
    a_up = noise(arg_keys[9], (D, R), D ** -0.5, 0.0625, ((0, 8),))
    gate_output_factor = noise(arg_keys[10], (R, FF), (4 * R) ** -0.5, 0.375, ((1, 64),))
    up_output_factor = noise(arg_keys[11], (R, FF), (4 * R) ** -0.5, 0.375, ((1, 64),))
    a_down = noise(arg_keys[12], (FF, R), FF ** -0.5, 0.03125, ((0, 64),))
    down_output_factor = noise(arg_keys[13], (R, D), (4 * R) ** -0.5, 0.375, ((1, 8),))
    return dict(tokens=tokens, cotangent=cotangent, rewards=rewards, group_ids=group_ids, token_mask=token_mask, w_gate=w_gate, w_up=w_up, down_weight_frozen=down_weight_frozen, a_gate=a_gate, a_up=a_up, gate_output_factor=gate_output_factor, up_output_factor=up_output_factor, a_down=a_down, down_output_factor=down_output_factor)


ADAPTER_SCALE = 2.0
KL_WEIGHT = 0.1


def frozen_product_rows(operand, weights):
    return jnp.dot(operand, weights, preferred_element_type=jnp.float32)


def trailing_inner_rows(operand, weights):
    return lax.dot_general(operand, weights, (((1,), (1,)), ((), ())), preferred_element_type=jnp.float32)


def leading_inner_rows(operand, weights):
    return lax.dot_general(operand, weights, (((0,), (0,)), ((), ())), preferred_element_type=jnp.float32)


def swish_parts(pre_gate):
    sigmoid = jax.nn.sigmoid(pre_gate)
    return pre_gate * sigmoid, sigmoid * (1.0 + pre_gate * (1.0 - sigmoid))


def reference(tokens, cotangent, rewards, group_ids, token_mask, w_gate, w_up, down_weight_frozen, a_gate, a_up, gate_output_factor, up_output_factor, a_down, down_output_factor):
    gate_frozen_rows = frozen_product_rows(tokens, w_gate)
    up_frozen_rows = frozen_product_rows(tokens, w_up)
    gate_adapter_factor = frozen_product_rows(tokens, a_gate).astype(jnp.bfloat16)
    up_adapter_factor = frozen_product_rows(tokens, a_up).astype(jnp.bfloat16)
    gate_policy_rows = gate_frozen_rows + ADAPTER_SCALE * frozen_product_rows(gate_adapter_factor, gate_output_factor)
    up_policy_rows = up_frozen_rows + ADAPTER_SCALE * frozen_product_rows(up_adapter_factor, up_output_factor)
    swish_policy, slope_policy = swish_parts(gate_policy_rows)
    swish_base, base_slope = swish_parts(gate_frozen_rows)
    policy_full = swish_policy * up_policy_rows
    hidden_policy = policy_full.astype(jnp.bfloat16)
    hidden_delta_rows = (policy_full - swish_base * up_frozen_rows).astype(jnp.bfloat16)
    down_adapter_factor = frozen_product_rows(hidden_policy, a_down).astype(jnp.bfloat16)
    output_delta_rows = frozen_product_rows(hidden_delta_rows, down_weight_frozen) + ADAPTER_SCALE * frozen_product_rows(down_adapter_factor, down_output_factor)
    divergence = 0.5 * jnp.mean(output_delta_rows * output_delta_rows, axis=1)
    mask_float = token_mask.astype(jnp.float32)
    membership = (group_ids[:, None] == jnp.arange(GROUPS, dtype=jnp.int32)[None, :]).astype(jnp.float32)
    group_reward = jnp.sum(membership * (mask_float * rewards)[:, None], axis=0)
    group_count = jnp.sum(membership * mask_float[:, None], axis=0)
    group_mean = group_reward / jnp.maximum(group_count, 1.0)
    advantage = rewards - jnp.sum(membership * group_mean[None, :], axis=1)
    token_scale = mask_float * (TOKENS / jnp.maximum(jnp.sum(group_count), 1.0))
    output_gradient_rows = (token_scale[:, None] * (KL_WEIGHT * output_delta_rows - advantage[:, None] * cotangent.astype(jnp.float32))).astype(jnp.bfloat16)
    down_output_gradient = ADAPTER_SCALE * leading_inner_rows(down_adapter_factor, output_gradient_rows)
    down_adapter_gradient = (ADAPTER_SCALE * trailing_inner_rows(output_gradient_rows, down_output_factor)).astype(jnp.bfloat16)
    grad_hidden = trailing_inner_rows(output_gradient_rows, down_weight_frozen) + trailing_inner_rows(down_adapter_gradient, a_down)
    grad_a_down = leading_inner_rows(hidden_policy, down_adapter_gradient)
    gate_gradient_rows = (grad_hidden * up_policy_rows * slope_policy).astype(jnp.bfloat16)
    up_gradient_rows = (grad_hidden * swish_policy).astype(jnp.bfloat16)
    gate_output_gradient = ADAPTER_SCALE * leading_inner_rows(gate_adapter_factor, gate_gradient_rows)
    up_output_gradient = ADAPTER_SCALE * leading_inner_rows(up_adapter_factor, up_gradient_rows)
    gate_adapter_gradient = (ADAPTER_SCALE * trailing_inner_rows(gate_gradient_rows, gate_output_factor)).astype(jnp.bfloat16)
    up_adapter_gradient = (ADAPTER_SCALE * trailing_inner_rows(up_gradient_rows, up_output_factor)).astype(jnp.bfloat16)
    grad_a_gate = leading_inner_rows(tokens, gate_adapter_gradient)
    grad_a_up = leading_inner_rows(tokens, up_adapter_gradient)
    grad_x = (trailing_inner_rows(gate_gradient_rows, w_gate) + trailing_inner_rows(up_gradient_rows, w_up) + trailing_inner_rows(gate_adapter_gradient, a_gate) + trailing_inner_rows(up_adapter_gradient, a_up)).astype(jnp.bfloat16)
    return (grad_x, divergence, grad_a_gate, grad_a_up, gate_output_gradient, up_output_gradient, grad_a_down, down_output_gradient)
```

```python
import functools

import jax
import jax.numpy as jnp
from jax import lax
from jax.experimental import pallas as pl
from jax.experimental.pallas import tpu as pltpu
from jax.sharding import PartitionSpec as P

MESH = pl.DeviceIdType.MESH
BF16 = jnp.bfloat16
F32 = jnp.float32
D = 8192
TOKENS = 256
RANK = 64
ADAPTER_SCALE = 2.0
KL_WEIGHT = 0.1
NQ = 8
LANES = 128


def mm(a, b):
    return jnp.dot(a, b, preferred_element_type=F32)


def mm_nt(a, b):
    return lax.dot_general(a, b, (((1,), (1,)), ((), ())), preferred_element_type=F32)


def mm_tn(a, b):
    return lax.dot_general(a, b, (((0,), (0,)), ((), ())), preferred_element_type=F32)


class Plan:
    def __init__(self, wide, narrow, db, fb):
        self.nc = 2
        self.nx = 4 if wide == 64 else 2
        self.ny = wide // (self.nx * self.nc)
        self.nz = narrow
        self.wide = wide
        self.db, self.fb = db, fb
        self.th = 2 * wide
        self.tz = self.th // narrow
        self.bs = min(16, wide)
        self.yb = self.bs // (self.nx * 2)
        self.names, self.shapes = [], []
        nx, ny, nz, th, tz = self.nx, self.ny, self.nz, self.th, self.tz
        zw = 2 * fb + LANES
        v = self.vmem
        v("wgu", (db, 2 * fb), BF16)
        v("down", (fb, db), BF16)
        v("ag", (db, RANK), BF16)
        v("au", (db, RANK), BF16)
        v("agu", (db, LANES), BF16)
        v("bd", (LANES, 2 * fb), BF16)
        v("adown", (fb, RANK), BF16)
        v("bdown", (RANK, db), BF16)
        v("tok", (4, db), BF16)
        v("cot", (4, db), BF16)
        v("t32", (2, 16, LANES), F32)
        v("c32", (2, 16, LANES), F32)
        v("o32", (4, db), F32)
        self.dma("load", 10)
        for h in range(2):
            k = str(h)
            for g in "AD":
                v(g + "g" + k, (ny, nx, 2, 16, LANES), BF16)
                self.rem(g + "y" + k, ny - 1)
                self.rem(g + "x" + k, nx - 1)
                self.rem(g + "c" + k, 1)
            for g in "CF":
                v(g + "r" + k, (ny, nx, 2, 16, LANES), BF16)
                v(g + "rc" + k, (ny, nx, 16, LANES), BF16)
                v(g + "s1" + k, (ny, nx, 16, LANES), BF16)
                v(g + "rx" + k, (nx - 1, ny, 16, LANES), BF16)
                v(g + "s2" + k, (ny, 16, LANES), BF16)
                v(g + "ry" + k, (ny - 1, 16, LANES), BF16)
                self.rem(g + "c" + k, 1)
                self.rem(g + "x" + k, nx - 1)
                self.rem(g + "y" + k, ny - 1)
            for g, width in (("B", zw), ("E", fb)):
                v(g + "b" + k, (nz, tz, width), BF16)
                v(g + "r" + k, (nz - 1, tz, width), BF16)
                v(g + "g" + k, (nz, tz, width), BF16)
                self.rem(g + "rs" + k, nz - 1)
                self.rem(g + "ag" + k, nz - 1)
            v("x" + k, (th, db), BF16)
            v("go" + k, (th, db), BF16)
            v("hp" + k, (th, fb), BF16)
            v("su" + k, (th, 2 * fb), F32)
            v("ggu" + k, (th, 2 * fb), BF16)
        for g, rows in (("fd", th), ("ad", 2 * th)):
            part = rows // 2 // nx
            v(g + "p", (2, nx, part, LANES), BF16)
            v(g + "rc", (nx, part, LANES), BF16)
            v(g + "s1", (nx, part, LANES), BF16)
            v(g + "rx", (nx - 1, part, LANES), BF16)
            v(g + "s2", (part, LANES), BF16)
            v(g + "ry", (ny - 1, part, LANES), BF16)
            v(g + "f", (2, nx, part, LANES), BF16)
            self.rem(g + "c", 1)
            self.rem(g + "x", nx - 1)
            self.rem(g + "y", ny - 1)
            self.rem(g + "X", nx - 1)
            self.rem(g + "C", 1)
        v("gfb", (nz, tz, LANES), BF16)
        v("gfr", (nz - 1, tz, LANES), BF16)
        v("gfg", (nz, tz, LANES), BF16)
        self.rem("gfrs", nz - 1)
        self.rem("gfag", nz - 1)
        for name in ("st0", "st1", "st2", "stc", "dv"):
            v(name, (8, LANES), F32)
        v("stx", (nx - 1, 8, LANES), F32)
        v("sty", (ny - 1, 8, LANES), F32)
        v("dvr", (nz - 1, 8, LANES), F32)
        self.rem("stc_", 1)
        self.rem("stx_", nx - 1)
        self.rem("sty_", ny - 1)
        self.rem("dv_", nz - 1)

    def vmem(self, name, shape, dtype):
        self.names.append(name)
        self.shapes.append(pltpu.VMEM(shape, dtype))

    def dma(self, name, count):
        self.names.append(name)
        self.shapes.append(pltpu.SemaphoreType.DMA((count,)))

    def rem(self, name, count):
        self.dma(name + ">", count)
        self.dma(name + "<", count)


def step_kernel(plan, *refs):
    (tokens, cotangent, rewards, group_ids, token_mask, w_gate, w_up, down_w, a_gate, a_up,
     gate_of, up_of, a_down, down_of) = refs[:14]
    (gx_o, dv_o, ad_o, x_o, gu_o, gad_o, dog_o) = refs[14:21]
    r = dict(zip(plan.names, refs[21:]))
    ny, nx, nz, th, tz, db, fb = plan.ny, plan.nx, plan.nz, plan.th, plan.tz, plan.db, plan.fb
    w = lax.axis_index("wide")
    z = lax.axis_index("narrow")
    y, x, c = w // (nx * 2), (w // 2) % nx, w % 2
    other = 1 - c

    def wide_of(yy, xx, cc):
        return (yy * nx + xx) * 2 + cc

    ys = [(y + d) % ny for d in range(1, ny)]
    xs = [(x + d) % nx for d in range(1, nx)]
    zs = [(z + d) % nz for d in range(1, nz)]
    dev_y = [(wide_of(v, x, c), z) for v in ys]
    dev_x = [(wide_of(y, v, c), z) for v in xs]
    dev_c = (wide_of(y, x, other), z)
    dev_z = [(w, v) for v in zs]
    peers = dev_y + dev_x + [dev_c] + dev_z

    barrier = pltpu.get_barrier_semaphore()
    for peer in peers:
        pl.semaphore_signal(barrier, inc=1, device_id=peer, device_id_type=MESH)

    loads = []
    for src, dst in (
        (tokens, r["tok"]), (w_gate, r["wgu"].at[:, :fb]), (w_up, r["wgu"].at[:, fb:]),
        (a_gate, r["ag"]), (a_up, r["au"]), (gate_of, r["bd"].at[:RANK, :fb]),
        (up_of, r["bd"].at[RANK:, fb:]), (cotangent, r["cot"]), (down_w, r["down"]),
        (a_down, r["adown"]),
    ):
        copy = pltpu.make_async_copy(src, dst, r["load"].at[len(loads)])
        copy.start()
        loads.append(copy)

    pending = []
    flying = {}

    def send(name, index, src, dst, device):
        copy = pltpu.make_async_remote_copy(
            src_ref=src, dst_ref=dst, send_sem=r[name + ">"].at[index],
            recv_sem=r[name + "<"].at[index], device_id=device, device_id_type=MESH,
        )
        copy.start()
        pending.append(copy)
        flying.setdefault(name, []).append(copy)

    def arrive(name):
        for copy in flying.pop(name):
            copy.wait_recv()

    def gather_y(g, k):
        buf = r[g + "g" + k]
        for i, device in enumerate(dev_y):
            send(g + "y" + k, i, buf.at[y, x, c], buf.at[y, x, c], device)

    def gather_x(g, k):
        buf = r[g + "g" + k]
        arrive(g + "y" + k)
        for i, device in enumerate(dev_x):
            send(g + "x" + k, i, buf.at[:, x, c], buf.at[:, x, c], device)

    def gather_c(g, k):
        buf = r[g + "g" + k]
        arrive(g + "x" + k)
        send(g + "c" + k, 0, buf.at[:, :, c], buf.at[:, :, c], dev_c)

    def scatter_c(g, k):
        buf = r[g + "r" + k]
        send(g + "c" + k, 0, buf.at[:, :, other], r[g + "rc" + k], dev_c)

    def scatter_x(g, k):
        arrive(g + "c" + k)
        total = r[g + "r" + k][:, :, c].astype(F32) + r[g + "rc" + k][...].astype(F32)
        r[g + "s1" + k][...] = total.astype(BF16)
        for i, device in enumerate(dev_x):
            send(g + "x" + k, i, r[g + "s1" + k].at[:, xs[i]], r[g + "rx" + k].at[i], device)

    def scatter_y(g, k):
        arrive(g + "x" + k)
        total = r[g + "s1" + k][:, x].astype(F32)
        for i in range(nx - 1):
            total += r[g + "rx" + k][i].astype(F32)
        r[g + "s2" + k][...] = total.astype(BF16)
        for i, device in enumerate(dev_y):
            send(g + "y" + k, i, r[g + "s2" + k].at[ys[i]], r[g + "ry" + k].at[i], device)

    def scatter_end(g, k):
        arrive(g + "y" + k)
        total = r[g + "s2" + k][y].astype(F32)
        for i in range(ny - 1):
            total += r[g + "ry" + k][i].astype(F32)
        return total

    def narrow_sum(b, g, k):
        for i, device in enumerate(dev_z):
            send(g + "rs" + k, i, r[b + k].at[zs[i]], r[g + "r" + k].at[i], device)

    def narrow_hand(b, g, k):
        arrive(g + "rs" + k)
        total = r[b + k][z].astype(F32)
        for i in range(nz - 1):
            total += r[g + "r" + k][i].astype(F32)
        r[g + "g" + k][z] = total.astype(BF16)
        for i, device in enumerate(dev_z):
            send(g + "ag" + k, i, r[g + "g" + k].at[z], r[g + "g" + k].at[z], device)

    def small_c(g):
        send(g + "c", 0, r[g + "p"].at[other], r[g + "rc"], dev_c)

    def small_x(g):
        arrive(g + "c")
        r[g + "s1"][...] = (r[g + "p"][c].astype(F32) + r[g + "rc"][...].astype(F32)).astype(BF16)
        for i, device in enumerate(dev_x):
            send(g + "x", i, r[g + "s1"].at[xs[i]], r[g + "rx"].at[i], device)

    def small_y(g):
        arrive(g + "x")
        total = r[g + "s1"][x].astype(F32)
        for i in range(nx - 1):
            total += r[g + "rx"][i].astype(F32)
        r[g + "s2"][...] = total.astype(BF16)
        for i, device in enumerate(dev_y):
            send(g + "y", i, r[g + "s2"], r[g + "ry"].at[i], device)

    def small_X(g):
        arrive(g + "y")
        total = r[g + "s2"][...].astype(F32)
        for i in range(ny - 1):
            total += r[g + "ry"][i].astype(F32)
        r[g + "f"][c, x] = total.astype(BF16)
        for i, device in enumerate(dev_x):
            send(g + "X", i, r[g + "f"].at[c, x], r[g + "f"].at[c, x], device)

    def small_C(g):
        arrive(g + "X")
        send(g + "C", 0, r[g + "f"].at[c], r[g + "f"].at[c], dev_c)

    rows = plan.bs * 16
    row = lax.broadcasted_iota(jnp.int32, (rows, rows), 0)
    col = lax.broadcasted_iota(jnp.int32, (rows, rows), 1)

    def by_block(v):
        return ((v >> 1) & 7) * (2 * plan.bs) + (v >> 4) * 2 + (v & 1)

    to_tokens = (row == by_block(col)).astype(F32).astype(BF16)
    to_shards = (col == by_block(row)).astype(F32).astype(BF16)

    def unpack(g, k, out):
        for b in range(plan.wide // plan.bs):
            block = r[g + "g" + k][plan.yb * b:plan.yb * (b + 1)].reshape(rows, LANES)
            turned = mm(to_tokens, block).astype(BF16)
            n = 2 * plan.bs
            for q in range(NQ):
                out[n * b:n * (b + 1), LANES * q:LANES * (q + 1)] = turned[n * q:n * (q + 1)]

    def pack(value, g, k):
        for b in range(plan.wide // plan.bs):
            n = 2 * plan.bs
            block = jnp.concatenate(
                [value[n * b:n * (b + 1), LANES * q:LANES * (q + 1)] for q in range(NQ)], axis=0)
            turned = mm(to_shards, block).astype(BF16)
            r[g + "r" + k][plan.yb * b:plan.yb * (b + 1)] = turned.reshape(
                plan.yb, nx, 2, 16, LANES)

    loads[0].wait()
    tok = r["tok"][...].astype(F32)
    for h in range(2):
        for q in range(NQ):
            r["t32"][h, 2 * q:2 * q + 2, :] = tok[2 * h:2 * h + 2, LANES * q:LANES * (q + 1)]
        r["Ag" + str(h)][y, x, c] = r["t32"][h].astype(BF16)

    pl.semaphore_wait(barrier, len(peers))
    gather_y("A", "0")
    gather_y("A", "1")

    lane = lax.broadcasted_iota(jnp.int32, (1, LANES), 1)
    mask = [token_mask[t].astype(F32) for t in range(4)]
    reward = [rewards[t] for t in range(4)]
    ids = [group_ids[t] for t in range(4)]
    reward_row = jnp.zeros((1, LANES), F32)
    count_row = jnp.zeros((1, LANES), F32)
    for t in range(4):
        reward_row += jnp.where(lane == ids[t], mask[t] * reward[t], 0.0)
        count_row += jnp.where(lane == ids[t], mask[t], 0.0)
    row8 = lax.broadcasted_iota(jnp.int32, (8, LANES), 0)
    r["st0"][...] = jnp.where(row8 == 0, reward_row, jnp.where(row8 == 1, count_row, 0.0))
    send("stc_", 0, r["st0"], r["stc"], dev_c)

    loads[7].wait()
    cot = r["cot"][...].astype(F32)
    for h in range(2):
        for q in range(NQ):
            r["c32"][h, 2 * q:2 * q + 2, :] = cot[2 * h:2 * h + 2, LANES * q:LANES * (q + 1)]
    for i in (3, 4, 5, 6):
        loads[i].wait()
    r["agu"][:, :RANK] = r["ag"][...]
    r["agu"][:, RANK:] = r["au"][...]
    r["bd"][:RANK, fb:] = jnp.zeros((RANK, fb), BF16)
    r["bd"][RANK:, :fb] = jnp.zeros((RANK, fb), BF16)
    bdown_load = pltpu.make_async_copy(down_of, r["bdown"], r["load"].at[0])
    bdown_load.start()

    arrive("stc_")
    r["st1"][...] = r["st0"][...] + r["stc"][...]
    for i, device in enumerate(dev_x):
        send("stx_", i, r["st1"], r["stx"].at[i], device)

    gather_x("A", "0")
    gather_x("A", "1")

    arrive("stx_")
    total = r["st1"][...]
    for i in range(nx - 1):
        total += r["stx"][i]
    r["st2"][...] = total
    for i, device in enumerate(dev_y):
        send("sty_", i, r["st2"], r["sty"].at[i], device)

    gather_c("A", "0")
    gather_c("A", "1")
    loads[1].wait()
    loads[2].wait()

    for h in range(2):
        k = str(h)
        arrive("Ac" + k)
        unpack("A", k, r["x" + k])
        xv = r["x" + k][...]
        r["Bb" + k][:, :, 2 * fb:] = mm(xv, r["agu"][...]).astype(BF16).reshape(nz, tz, LANES)
        r["Bb" + k][:, :, :2 * fb] = mm(xv, r["wgu"][...]).astype(BF16).reshape(nz, tz, 2 * fb)
        narrow_sum("Bb", "B", k)

    arrive("sty_")
    stats = r["st2"][...]
    for i in range(ny - 1):
        stats += r["sty"][i]
    group_count = stats[1:2]
    group_mean = stats[0:1] / jnp.maximum(group_count, 1.0)
    all_count = jnp.sum(group_count, axis=1, keepdims=True)
    scale_of = TOKENS / jnp.maximum(all_count, 1.0)
    advantage, token_scale = [], []
    for t in range(4):
        mean_t = jnp.sum(jnp.where(lane == ids[t], group_mean, 0.0), axis=1, keepdims=True)
        advantage.append(reward[t] - mean_t)
        token_scale.append(mask[t] * scale_of)

    narrow_hand("Bb", "B", "0")
    narrow_hand("Bb", "B", "1")
    loads[8].wait()
    loads[9].wait()
    bdown_load.wait()

    fd_parts = []
    for h in range(2):
        k = str(h)
        arrive("Bag" + k)
        both = r["Bg" + k][...].reshape(th, 2 * fb + LANES)
        adapt = ADAPTER_SCALE * mm(both[:, 2 * fb:], r["bd"][...])
        gate_base = both[:, :fb].astype(F32)
        up_base = both[:, fb:2 * fb].astype(F32)
        gate = gate_base + adapt[:, :fb]
        up = up_base + adapt[:, fb:]
        sig = jax.nn.sigmoid(gate)
        silu = gate * sig
        slope = sig * (1.0 + gate * (1.0 - sig))
        full = silu * up
        hp = full.astype(BF16)
        hd = (full - gate_base * jax.nn.sigmoid(gate_base) * up_base).astype(BF16)
        r["hp" + k][...] = hp
        r["su" + k][:, :fb] = up * slope
        r["su" + k][:, fb:] = silu
        fd = mm(hp, r["adown"][...])
        fd_parts.append(fd)
        out = mm(hd, r["down"][...]) + ADAPTER_SCALE * mm(fd.astype(BF16), r["bdown"][...])
        pack(out.astype(BF16), "C", k)
        scatter_c("C", k)
    fd_both = jnp.concatenate(fd_parts, axis=1).astype(BF16)
    r["fdp"][...] = fd_both.reshape(2, nx, th // 2 // nx, LANES)
    small_c("fd")

    scatter_x("C", "0")
    scatter_x("C", "1")
    small_x("fd")
    scatter_y("C", "0")
    scatter_y("C", "1")
    small_y("fd")

    row16 = lax.broadcasted_iota(jnp.int32, (16, 1), 0)
    even = (row16 & 1) == 0
    div = []
    for h in range(2):
        k = str(h)
        od = scatter_end("C", k)
        square = od * od
        for t in range(2):
            picked = jnp.where(((row16 & 1) == t), square, 0.0)
            div.append(jnp.sum(jnp.sum(picked, axis=1, keepdims=True), axis=0, keepdims=True))
        adv = jnp.where(even, advantage[2 * h], advantage[2 * h + 1])
        scl = jnp.where(even, token_scale[2 * h], token_scale[2 * h + 1])
        grad = scl * (KL_WEIGHT * od - adv * r["c32"][h])
        r["Dg" + k][y, x, c] = grad.astype(BF16)
        gather_y("D", k)
    dv = jnp.zeros((8, LANES), F32)
    for t in range(4):
        dv += jnp.where(row8 == t, div[t], 0.0)
    r["dv"][...] = dv * (0.5 / D)
    for i, device in enumerate(dev_z):
        send("dv_", i, r["dv"], r["dvr"].at[i], device)
    small_X("fd")
    gather_x("D", "0")
    gather_x("D", "1")
    small_C("fd")
    gather_c("D", "0")
    gather_c("D", "1")

    gf_parts = []
    for h in range(2):
        k = str(h)
        arrive("Dc" + k)
        unpack("D", k, r["go" + k])
        go = r["go" + k][...]
        gf = ADAPTER_SCALE * mm_nt(go, r["bdown"][...])
        gf_parts.append(gf)
        gh = mm_nt(go, r["down"][...]) + mm_nt(gf.astype(BF16), r["adown"][...])
        r["Eb" + k][...] = gh.astype(BF16).reshape(nz, tz, fb)
        narrow_sum("Eb", "E", k)
    gf_both = jnp.concatenate(gf_parts, axis=1).astype(BF16)
    r["gfb"][...] = gf_both.reshape(nz, tz, LANES)
    for i, device in enumerate(dev_z):
        send("gfrs", i, r["gfb"].at[zs[i]], r["gfr"].at[i], device)

    narrow_hand("Eb", "E", "0")
    narrow_hand("Eb", "E", "1")
    arrive("gfrs")
    total = r["gfb"][z].astype(F32)
    for i in range(nz - 1):
        total += r["gfr"][i].astype(F32)
    r["gfg"][z] = total.astype(BF16)
    for i, device in enumerate(dev_z):
        send("gfag", i, r["gfg"].at[z], r["gfg"].at[z], device)

    half = th // 2 // nx * 2
    for h in range(2):
        k = str(h)
        arrive("Eag" + k)
        gh = r["Eg" + k][...].reshape(th, fb).astype(F32)
        r["ggu" + k][:, :fb] = (gh * r["su" + k][:, :fb]).astype(BF16)
        r["ggu" + k][:, fb:] = (gh * r["su" + k][:, fb:]).astype(BF16)
        ggu = r["ggu" + k][...]
        ad = (ADAPTER_SCALE * mm_nt(ggu, r["bd"][...])).astype(BF16)
        r["adp"][h] = ad.reshape(nx, half, LANES)
        gx = mm_nt(ggu, r["wgu"][...]) + mm_nt(ad, r["agu"][...])
        pack(gx.astype(BF16), "F", k)
        scatter_c("F", k)
    small_c("ad")

    scatter_x("F", "0")
    scatter_x("F", "1")
    small_x("ad")
    gu = jnp.zeros((LANES, 2 * fb), F32)
    for h in range(2):
        k = str(h)
        factors = r["Bg" + k][:, :, 2 * fb:].reshape(th, LANES)
        gu += mm_tn(factors, r["ggu" + k][...])
    gu_o[...] = ADAPTER_SCALE * gu
    scatter_y("F", "0")
    scatter_y("F", "1")
    small_y("ad")

    arrive("fdC")
    fdf = r["fdf"][...].reshape(th, LANES)
    dog = mm_tn(fdf, r["go0"][...])[:RANK] + mm_tn(fdf, r["go1"][...])[RANK:]
    dog_o[...] = ADAPTER_SCALE * dog
    arrive("gfag")
    gff = r["gfg"][...].reshape(th, LANES)
    gad_o[...] = mm_tn(r["hp0"][...], gff)[:, :RANK] + mm_tn(r["hp1"][...], gff)[:, RANK:]
    arrive("dv_")
    total = r["dv"][...]
    for i in range(nz - 1):
        total += r["dvr"][i]
    dv_o[...] = total
    small_X("ad")
    for h in range(2):
        k = str(h)
        gx = scatter_end("F", k)
        for q in range(NQ):
            r["o32"][2 * h:2 * h + 2, LANES * q:LANES * (q + 1)] = gx[2 * q:2 * q + 2]
    gx_o[...] = r["o32"][...].astype(BF16)
    small_C("ad")
    for h in range(2):
        x_o[h * th:(h + 1) * th] = r["x" + str(h)][...]
    arrive("adC")
    ad_o[...] = r["adf"][...].reshape(2 * th, LANES)

    for copy in pending:
        copy.wait_send()


def finish_kernel(fb, gx, dv, ad, xv, gu, gad, dog, gx_o, dv_o, ag_o, au_o, gog_o, uog_o, gad_o,
                  dog_o):
    both = mm_tn(xv[...], ad[...])
    ag_o[...] = both[:, :RANK]
    au_o[...] = both[:, RANK:]
    gx_o[...] = gx[...]
    for t in range(4):
        dv_o[t] = jnp.max(dv[t:t + 1, :])
    gog_o[...] = gu[:RANK, :fb]
    uog_o[...] = gu[RANK:, fb:]
    gad_o[...] = gad[...]
    dog_o[...] = dog[...]


def shards(wide, narrow, tokens, cotangent, rewards, group_ids, token_mask, w_gate, w_up, down_w,
           a_gate, a_up, gate_of, up_of, a_down, down_of):
    db, fb = w_gate.shape
    plan = Plan(wide, narrow, db, fb)
    anyspace = pl.BlockSpec(memory_space=pl.ANY)
    vm = pl.BlockSpec(memory_space=pltpu.VMEM)
    sm = pl.BlockSpec(memory_space=pltpu.SMEM)
    s = jax.ShapeDtypeStruct
    mids = pl.pallas_call(
        functools.partial(step_kernel, plan),
        out_shape=(
            s((4, db), BF16), s((8, LANES), F32), s((2 * plan.th, LANES), BF16),
            s((2 * plan.th, db), BF16), s((LANES, 2 * fb), F32), s((fb, RANK), F32),
            s((RANK, db), F32),
        ),
        in_specs=[anyspace, anyspace, sm, sm, sm] + [anyspace] * 9,
        out_specs=(vm,) * 7,
        scratch_shapes=plan.shapes,
        compiler_params=pltpu.CompilerParams(
            collective_id=0, has_side_effects=True, vmem_limit_bytes=48 << 20),
        name="policy_step",
    )(tokens, cotangent, rewards, group_ids, token_mask, w_gate, w_up, down_w, a_gate, a_up,
      gate_of, up_of, a_down, down_of)
    outs = pl.pallas_call(
        functools.partial(finish_kernel, fb),
        out_shape=(
            s((4, db), BF16), s((4,), F32), s((db, RANK), F32), s((db, RANK), F32),
            s((RANK, fb), F32), s((RANK, fb), F32), s((fb, RANK), F32), s((RANK, db), F32),
        ),
        in_specs=[vm] * 7,
        out_specs=(vm, sm) + (vm,) * 6,
        compiler_params=pltpu.CompilerParams(vmem_limit_bytes=32 << 20),
        name="finish",
    )(*mids)
    return outs


def solution(mesh):
    return jax.shard_map(
        functools.partial(shards, mesh.shape["wide"], mesh.shape["narrow"]),
        mesh=mesh,
        in_specs=(
            P("wide", "narrow"),
            P("wide", "narrow"),
            P("wide"),
            P("wide"),
            P("wide"),
            P("narrow", "wide"),
            P("narrow", "wide"),
            P("wide", "narrow"),
            P("narrow", None),
            P("narrow", None),
            P(None, "wide"),
            P(None, "wide"),
            P("wide", None),
            P(None, "narrow"),
        ),
        out_specs=(
            P("wide", "narrow"),
            P("wide"),
            P("narrow", None),
            P("narrow", None),
            P(None, "wide"),
            P(None, "wide"),
            P("wide", None),
            P(None, "narrow"),
        ),
        check_vma=False,
    )
```

```python
import functools

import jax
import jax.numpy as jnp
from jax import lax
from jax.experimental import pallas as pl
from jax.experimental.pallas import tpu as pltpu
from jax.sharding import PartitionSpec as P

MESH = pl.DeviceIdType.MESH
BF16 = jnp.bfloat16
F32 = jnp.float32
D = 8192
TOKENS = 256
RANK = 64
ADAPTER_SCALE = 2.0
KL_WEIGHT = 0.1
NQ = 8
LANES = 128


def mm(a, b):
    return jnp.dot(a, b, preferred_element_type=F32)


def mm_nt(a, b):
    return lax.dot_general(a, b, (((1,), (1,)), ((), ())), preferred_element_type=F32)


def mm_tn(a, b):
    return lax.dot_general(a, b, (((0,), (0,)), ((), ())), preferred_element_type=F32)


class Plan:
    def __init__(self, wide, narrow, db, fb):
        self.nx = 4 if wide == 64 else 2
        self.ny = wide // (self.nx * 2)
        self.ne = 2 * self.nx
        self.nz = narrow
        self.wide = wide
        self.db, self.fb = db, fb
        self.th = 2 * wide
        self.tz = self.th // narrow
        self.bs = min(16, wide)
        self.yb = self.bs // self.ne
        self.names, self.shapes = [], []
        nx, ny, nz, ne, th, tz = self.nx, self.ny, self.nz, self.ne, self.th, self.tz
        v = self.vmem
        v("wgu", (db, 2 * fb), BF16)
        v("downx", (fb + LANES, db), BF16)
        v("agu", (LANES, db), BF16)
        v("bd", (LANES, 2 * fb), BF16)
        v("adown", (RANK, fb), BF16)
        v("tok", (4, db), BF16)
        v("cot", (4, db), BF16)
        v("t32", (2, 16, LANES), F32)
        v("c32", (2, 16, LANES), F32)
        v("o32", (4, db), F32)
        v("x", (2 * th, db), BF16)
        v("gx", (4, db), BF16)
        v("gab", (LANES, db), F32)
        v("gu", (LANES, 2 * fb), F32)
        v("gad", (RANK, fb), F32)
        v("dog", (RANK, db), F32)
        self.dma("load", 11)
        self.dma("out", 7)
        for h in range(2):
            k = str(h)
            for g in "AD":
                v(g + "g" + k, (ny, nx, 2, 16, LANES), BF16)
                self.rem(g + "y" + k, ny - 1)
                self.rem(g + "x" + k, nx - 1)
                self.rem(g + "c" + k, 1)
            for g in "CF":
                v(g + "r" + k, (ny, nx, 2, 16, LANES), BF16)
                v(g + "rc" + k, (ny, nx, 16, LANES), BF16)
                v(g + "s1" + k, (ny, nx, 16, LANES), BF16)
                v(g + "rx" + k, (nx - 1, ny, 16, LANES), BF16)
                v(g + "s2" + k, (ny, 16, LANES), BF16)
                v(g + "ry" + k, (ny - 1, 16, LANES), BF16)
                self.rem(g + "c" + k, 1)
                self.rem(g + "x" + k, nx - 1)
                self.rem(g + "y" + k, ny - 1)
            for g, width in (("B", 2 * fb + LANES), ("E", fb)):
                v(g + "b" + k, (nz, tz, width), BF16)
                v(g + "r" + k, (nz - 1, tz, width), BF16)
                self.rem(g + "rs" + k, nz - 1)
            for g, width in (("H", fb + LANES), ("K", 3 * fb + LANES), ("E", fb)):
                v(g + "g" + k, (nz, tz, width), BF16)
                self.rem(g + "ag" + k, nz - 1)
            v("go" + k, (th, db), BF16)
            v("ggu" + k, (th, 2 * fb), BF16)
        for g, rows in (("fd", th), ("ad", 2 * th)):
            part = rows // ne
            v(g + "p", (ne, part, LANES), BF16)
            v(g + "re", (ne - 1, part, LANES), BF16)
            v(g + "s", (part, LANES), BF16)
            v(g + "ry", (ny - 1, part, LANES), BF16)
            v(g + "f", (ne, part, LANES), BF16)
            self.rem(g + "e", ne - 1)
            self.rem(g + "y", ny - 1)
            self.rem(g + "E", ne - 1)
        v("Gb", (nz, tz, LANES), BF16)
        v("Gr", (nz - 1, tz, LANES), BF16)
        v("Gg", (nz, tz, LANES), BF16)
        self.rem("Grs", nz - 1)
        self.rem("Gag", nz - 1)
        for name in ("st0", "st1", "dv"):
            v(name, (8, LANES), F32)
        v("ste", (ne - 1, 8, LANES), F32)
        v("sty", (ny - 1, 8, LANES), F32)
        v("dvr", (nz - 1, 8, LANES), F32)
        self.rem("ste_", ne - 1)
        self.rem("sty_", ny - 1)
        self.rem("dv_", nz - 1)

    def vmem(self, name, shape, dtype):
        self.names.append(name)
        self.shapes.append(pltpu.VMEM(shape, dtype))

    def dma(self, name, count):
        self.names.append(name)
        self.shapes.append(pltpu.SemaphoreType.DMA((count,)))

    def rem(self, name, count):
        self.dma(name + ">", count)
        self.dma(name + "<", count)


def step_kernel(plan, *refs):
    (tokens, cotangent, rewards, group_ids, token_mask, w_gate, w_up, down_w, a_gate, a_up,
     gate_of, up_of, a_down, down_of) = refs[:14]
    (gx_o, dv_o, ag_o, au_o, gog_o, uog_o, gad_o, dog_o) = refs[14:22]
    r = dict(zip(plan.names, refs[22:]))
    ny, nx, nz, ne, th, tz, db, fb = (
        plan.ny, plan.nx, plan.nz, plan.ne, plan.th, plan.tz, plan.db, plan.fb)
    w = lax.axis_index("wide")
    z = lax.axis_index("narrow")
    y, x, c = w // ne, (w // 2) % nx, w % 2
    e = w % ne
    other = 1 - c

    ys = [(y + d) % ny for d in range(1, ny)]
    xs = [(x + d) % nx for d in range(1, nx)]
    es = [(e + d) % ne for d in range(1, ne)]
    zs = [(z + d) % nz for d in range(1, nz)]
    dev_y = [(v * ne + e, z) for v in ys]
    dev_x = [(y * ne + v * 2 + c, z) for v in xs]
    dev_e = [(y * ne + v, z) for v in es]
    dev_c = (y * ne + x * 2 + other, z)
    dev_z = [(w, v) for v in zs]
    peers = dev_y + dev_e + dev_z

    barrier = pltpu.get_barrier_semaphore()
    for peer in peers:
        pl.semaphore_signal(barrier, inc=1, device_id=peer, device_id_type=MESH)

    loads = []
    for src, dst in (
        (tokens, r["tok"]), (w_gate, r["wgu"].at[:, :fb]), (w_up, r["wgu"].at[:, fb:]),
        (a_gate, r["agu"].at[:RANK]), (a_up, r["agu"].at[RANK:]),
        (gate_of, r["bd"].at[:RANK, :fb]), (up_of, r["bd"].at[RANK:, fb:]),
        (cotangent, r["cot"]), (down_w, r["downx"].at[:fb]),
        (down_of, r["downx"].at[fb:fb + RANK]), (down_of, r["downx"].at[fb + RANK:]),
    ):
        copy = pltpu.make_async_copy(src, dst, r["load"].at[len(loads)])
        copy.start()
        loads.append(copy)

    pending = []
    flying = {}
    stores = []

    def store(src, dst):
        copy = pltpu.make_async_copy(src, dst, r["out"].at[len(stores)])
        copy.start()
        stores.append(copy)

    def send(name, index, src, dst, device):
        copy = pltpu.make_async_remote_copy(
            src_ref=src, dst_ref=dst, send_sem=r[name + ">"].at[index],
            recv_sem=r[name + "<"].at[index], device_id=device, device_id_type=MESH,
        )
        copy.start()
        pending.append(copy)
        flying.setdefault(name, []).append(copy)

    def arrive(name):
        for copy in flying.pop(name):
            copy.wait_recv()

    def add_up(total, slots, count):
        total = total.astype(F32)
        for i in range(count):
            total += slots[i].astype(F32)
        return total

    def gather_y(g, k):
        buf = r[g + "g" + k]
        for i, device in enumerate(dev_y):
            send(g + "y" + k, i, buf.at[y, x, c], buf.at[y, x, c], device)

    def gather_x(g, k):
        buf = r[g + "g" + k]
        arrive(g + "y" + k)
        for i, device in enumerate(dev_x):
            send(g + "x" + k, i, buf.at[:, x, c], buf.at[:, x, c], device)

    def gather_c(g, k):
        buf = r[g + "g" + k]
        arrive(g + "x" + k)
        send(g + "c" + k, 0, buf.at[:, :, c], buf.at[:, :, c], dev_c)

    def scatter_c(g, k):
        buf = r[g + "r" + k]
        send(g + "c" + k, 0, buf.at[:, :, other], r[g + "rc" + k], dev_c)

    def scatter_x(g, k):
        arrive(g + "c" + k)
        total = r[g + "r" + k][:, :, c].astype(F32) + r[g + "rc" + k][...].astype(F32)
        r[g + "s1" + k][...] = total.astype(BF16)
        for i, device in enumerate(dev_x):
            send(g + "x" + k, i, r[g + "s1" + k].at[:, xs[i]], r[g + "rx" + k].at[i], device)

    def scatter_y(g, k):
        arrive(g + "x" + k)
        total = add_up(r[g + "s1" + k][:, x], r[g + "rx" + k], nx - 1)
        r[g + "s2" + k][...] = total.astype(BF16)
        for i, device in enumerate(dev_y):
            send(g + "y" + k, i, r[g + "s2" + k].at[ys[i]], r[g + "ry" + k].at[i], device)

    def scatter_end(g, k):
        arrive(g + "y" + k)
        return add_up(r[g + "s2" + k][y], r[g + "ry" + k], ny - 1)

    def narrow_sum(g, k):
        for i, device in enumerate(dev_z):
            send(g + "rs" + k, i, r[g + "b" + k].at[zs[i]], r[g + "r" + k].at[i], device)

    def narrow_total(g, k):
        arrive(g + "rs" + k)
        return add_up(r[g + "b" + k][z], r[g + "r" + k], nz - 1)

    def narrow_hand(g, k):
        for i, device in enumerate(dev_z):
            send(g + "ag" + k, i, r[g + "g" + k].at[z], r[g + "g" + k].at[z], device)

    def small_row(g):
        for i, device in enumerate(dev_e):
            send(g + "e", i, r[g + "p"].at[es[i]], r[g + "re"].at[i], device)

    def small_y(g):
        arrive(g + "e")
        r[g + "s"][...] = add_up(r[g + "p"][e], r[g + "re"], ne - 1).astype(BF16)
        for i, device in enumerate(dev_y):
            send(g + "y", i, r[g + "s"], r[g + "ry"].at[i], device)

    def small_hand(g):
        arrive(g + "y")
        r[g + "f"][e] = add_up(r[g + "s"][...], r[g + "ry"], ny - 1).astype(BF16)
        for i, device in enumerate(dev_e):
            send(g + "E", i, r[g + "f"].at[e], r[g + "f"].at[e], device)

    rows = plan.bs * 16
    row = lax.broadcasted_iota(jnp.int32, (rows, rows), 0)
    col = lax.broadcasted_iota(jnp.int32, (rows, rows), 1)

    def by_block(v):
        return ((v >> 1) & 7) * (2 * plan.bs) + (v >> 4) * 2 + (v & 1)

    to_tokens = (row == by_block(col)).astype(F32).astype(BF16)
    to_shards = (col == by_block(row)).astype(F32).astype(BF16)

    def unpack(g, k, out, base):
        for b in range(plan.wide // plan.bs):
            block = r[g + "g" + k][plan.yb * b:plan.yb * (b + 1)].reshape(rows, LANES)
            turned = mm(to_tokens, block).astype(BF16)
            n = 2 * plan.bs
            for q in range(NQ):
                out[base + n * b:base + n * (b + 1), LANES * q:LANES * (q + 1)] = (
                    turned[n * q:n * (q + 1)])

    def pack(value, g, k):
        for b in range(plan.wide // plan.bs):
            n = 2 * plan.bs
            block = jnp.concatenate(
                [value[n * b:n * (b + 1), LANES * q:LANES * (q + 1)] for q in range(NQ)], axis=0)
            turned = mm(to_shards, block).astype(BF16)
            r[g + "r" + k][plan.yb * b:plan.yb * (b + 1)] = turned.reshape(
                plan.yb, nx, 2, 16, LANES)

    loads[0].wait()
    tok = r["tok"][...].astype(F32)
    for h in range(2):
        for q in range(NQ):
            r["t32"][h, 2 * q:2 * q + 2, :] = tok[2 * h:2 * h + 2, LANES * q:LANES * (q + 1)]
        r["Ag" + str(h)][y, x, c] = r["t32"][h].astype(BF16)

    lane = lax.broadcasted_iota(jnp.int32, (1, LANES), 1)
    mask = [token_mask[t].astype(F32) for t in range(4)]
    reward = [rewards[t] for t in range(4)]
    ids = [group_ids[t] for t in range(4)]
    reward_row = jnp.zeros((1, LANES), F32)
    count_row = jnp.zeros((1, LANES), F32)
    for t in range(4):
        reward_row += jnp.where(lane == ids[t], mask[t] * reward[t], 0.0)
        count_row += jnp.where(lane == ids[t], mask[t], 0.0)
    row8 = lax.broadcasted_iota(jnp.int32, (8, LANES), 0)
    r["st0"][...] = jnp.where(row8 == 0, reward_row, jnp.where(row8 == 1, count_row, 0.0))

    pl.semaphore_wait(barrier, len(peers))
    gather_y("A", "0")
    gather_y("A", "1")
    for i, device in enumerate(dev_e):
        send("ste_", i, r["st0"], r["ste"].at[i], device)
    loads[7].wait()
    cot = r["cot"][...].astype(F32)
    for h in range(2):
        for q in range(NQ):
            r["c32"][h, 2 * q:2 * q + 2, :] = cot[2 * h:2 * h + 2, LANES * q:LANES * (q + 1)]
    r["bd"][:RANK, fb:] = jnp.zeros((RANK, fb), BF16)
    r["bd"][RANK:, :fb] = jnp.zeros((RANK, fb), BF16)
    loads[0] = pltpu.make_async_copy(a_down, r["adown"], r["load"].at[0])
    loads[0].start()
    gather_x("A", "0")
    gather_x("A", "1")

    arrive("ste_")
    r["st1"][...] = add_up(r["st0"][...], r["ste"], ne - 1)
    for i, device in enumerate(dev_y):
        send("sty_", i, r["st1"], r["sty"].at[i], device)
    for i in (1, 2, 3, 4, 5, 6):
        loads[i].wait()
    gather_c("A", "0")
    gather_c("A", "1")

    def project(h):
        k = str(h)
        arrive("Ac" + k)
        unpack("A", k, r["x"], h * th)
        xv = r["x"][h * th:(h + 1) * th]
        r["Bb" + k][:, :, 2 * fb:] = (
            mm_nt(xv, r["agu"][...]).astype(BF16).reshape(nz, tz, LANES))
        r["Bb" + k][:, :, :2 * fb] = (
            mm(xv, r["wgu"][...]).astype(BF16).reshape(nz, tz, 2 * fb))
        narrow_sum("B", k)

    project(0)
    project(1)

    arrive("sty_")
    stats = add_up(r["st1"][...], r["sty"], ny - 1)
    group_count = stats[1:2]
    group_mean = stats[0:1] / jnp.maximum(group_count, 1.0)
    all_count = jnp.sum(group_count, axis=1, keepdims=True)
    scale_of = TOKENS / jnp.maximum(all_count, 1.0)
    advantage, token_scale = [], []
    for t in range(4):
        mean_t = jnp.sum(jnp.where(lane == ids[t], group_mean, 0.0), axis=1, keepdims=True)
        advantage.append(reward[t] - mean_t)
        token_scale.append(mask[t] * scale_of)
    loads[0].wait()

    def hidden(h):
        k = str(h)
        total = narrow_total("B", k)
        factors = total[:, 2 * fb:].astype(BF16)
        adapt = ADAPTER_SCALE * mm(factors, r["bd"][...])
        gate_base = total[:, :fb]
        up_base = total[:, fb:2 * fb]
        gate = gate_base + adapt[:, :fb]
        up = up_base + adapt[:, fb:]
        sig = jax.nn.sigmoid(gate)
        silu = gate * sig
        slope = sig * (1.0 + gate * (1.0 - sig))
        full = silu * up
        hp = full.astype(BF16)
        hd = (full - gate_base * jax.nn.sigmoid(gate_base) * up_base).astype(BF16)
        fd = ADAPTER_SCALE * mm_nt(hp, r["adown"][...])
        none = jnp.zeros_like(fd)
        fd = jnp.concatenate([none, fd] if h else [fd, none], axis=1)
        r["Hg" + k][z, :, :fb] = hd
        r["Hg" + k][z, :, fb:] = fd.astype(BF16)
        narrow_hand("H", k)
        r["Kg" + k][z, :, :fb] = (up * slope).astype(BF16)
        r["Kg" + k][z, :, fb:2 * fb] = silu.astype(BF16)
        r["Kg" + k][z, :, 2 * fb:3 * fb] = hp
        r["Kg" + k][z, :, 3 * fb:] = factors

    hidden(0)
    hidden(1)
    narrow_hand("K", "0")
    narrow_hand("K", "1")
    for i in (8, 9, 10):
        loads[i].wait()

    def outward(h):
        k = str(h)
        arrive("Hag" + k)
        both = r["Hg" + k][...].reshape(th, fb + LANES)
        pack(mm(both, r["downx"][...]).astype(BF16), "C", k)
        scatter_c("C", k)
        return both[:, fb:].astype(F32)

    row16 = lax.broadcasted_iota(jnp.int32, (16, 1), 0)
    even = (row16 & 1) == 0
    div = []

    def gradient(h):
        k = str(h)
        od = scatter_end("C", k)
        adv = jnp.where(even, advantage[2 * h], advantage[2 * h + 1])
        scl = jnp.where(even, token_scale[2 * h], token_scale[2 * h + 1])
        grad = scl * (KL_WEIGHT * od - adv * r["c32"][h])
        r["Dg" + k][y, x, c] = grad.astype(BF16)
        gather_y("D", k)
        square = od * od
        for t in range(2):
            picked = jnp.where(((row16 & 1) == t), square, 0.0)
            div.append(jnp.sum(jnp.sum(picked, axis=1, keepdims=True), axis=0, keepdims=True))

    fd0 = outward(0)
    scatter_x("C", "0")
    fd1 = outward(1)
    r["fdp"][...] = (fd0 + fd1).astype(BF16).reshape(ne, th // ne, LANES)
    small_row("fd")
    scatter_y("C", "0")
    scatter_x("C", "1")
    gradient(0)
    scatter_y("C", "1")
    small_y("fd")
    gather_x("D", "0")
    gradient(1)
    dv = jnp.zeros((8, LANES), F32)
    for t in range(4):
        dv += jnp.where(row8 == t, div[t], 0.0)
    r["dv"][...] = dv * (0.5 / D)
    for i, device in enumerate(dev_z):
        send("dv_", i, r["dv"], r["dvr"].at[i], device)
    gather_c("D", "0")
    gather_x("D", "1")
    small_hand("fd")

    def inward(h):
        k = str(h)
        arrive("Dc" + k)
        unpack("D", k, r["go" + k], 0)
        both = mm_nt(r["go" + k][...], r["downx"][...])
        gf = ADAPTER_SCALE * both[:, fb:]
        gh = both[:, :fb] + mm(gf[:, :RANK].astype(BF16), r["adown"][...])
        r["Eb" + k][...] = gh.astype(BF16).reshape(nz, tz, fb)
        narrow_sum("E", k)
        return gf

    gf0 = inward(0)
    gather_c("D", "1")
    gf1 = inward(1)
    r["Gb"][...] = jnp.where(lane < RANK, gf0, gf1).astype(BF16).reshape(nz, tz, LANES)
    for i, device in enumerate(dev_z):
        send("Grs", i, r["Gb"].at[zs[i]], r["Gr"].at[i], device)
    r["Eg0"][z] = narrow_total("E", "0").astype(BF16)
    narrow_hand("E", "0")
    arrive("fdE")
    fdf = r["fdf"][...].reshape(th, LANES)
    r["dog"][...] = mm_tn(fdf, r["go0"][...])[:RANK] + mm_tn(fdf, r["go1"][...])[RANK:]
    store(r["dog"], dog_o)
    r["Eg1"][z] = narrow_total("E", "1").astype(BF16)
    narrow_hand("E", "1")
    arrive("Grs")
    r["Gg"][z] = add_up(r["Gb"][z], r["Gr"], nz - 1).astype(BF16)
    for i, device in enumerate(dev_z):
        send("Gag", i, r["Gg"].at[z], r["Gg"].at[z], device)
    arrive("Kag0")
    arrive("Kag1")

    def back(h):
        k = str(h)
        arrive("Eag" + k)
        gh = r["Eg" + k][...].reshape(th, fb).astype(F32)
        kept = r["Kg" + k][...].reshape(th, 3 * fb + LANES)
        r["ggu" + k][:, :fb] = (gh * kept[:, :fb].astype(F32)).astype(BF16)
        r["ggu" + k][:, fb:] = (gh * kept[:, fb:2 * fb].astype(F32)).astype(BF16)
        ggu = r["ggu" + k][...]
        ad = (ADAPTER_SCALE * mm_nt(ggu, r["bd"][...])).astype(BF16)
        r["adp"][h * nx:(h + 1) * nx] = ad.reshape(nx, 2 * th // ne, LANES)
        if h == 1:
            small_row("ad")
        gx = mm_nt(ggu, r["wgu"][...]) + mm(ad, r["agu"][...])
        pack(gx.astype(BF16), "F", k)
        scatter_c("F", k)

    back(0)
    scatter_x("F", "0")
    back(1)
    scatter_y("F", "0")
    scatter_x("F", "1")
    small_y("ad")
    gu = jnp.zeros((LANES, 2 * fb), F32)
    for h in range(2):
        k = str(h)
        factors = r["Kg" + k][:, :, 3 * fb:].reshape(th, LANES)
        gu += mm_tn(factors, r["ggu" + k][...])
    r["gu"][...] = ADAPTER_SCALE * gu
    store(r["gu"].at[:RANK, :fb], gog_o)
    store(r["gu"].at[RANK:, fb:], uog_o)

    def input_gradient(h):
        gx = scatter_end("F", str(h))
        for q in range(NQ):
            r["o32"][2 * h:2 * h + 2, LANES * q:LANES * (q + 1)] = gx[2 * q:2 * q + 2]

    scatter_y("F", "1")
    small_hand("ad")
    input_gradient(0)
    arrive("Gag")
    gff = r["Gg"][...].reshape(th, LANES)
    parts = [mm_tn(gff, r["Kg" + k][:, :, 2 * fb:3 * fb].reshape(th, fb)) for k in "01"]
    r["gad"][...] = parts[0][:RANK] + parts[1][RANK:]
    store(r["gad"], gad_o)
    arrive("dv_")
    dv = add_up(r["dv"][...], r["dvr"], nz - 1)
    for t in range(4):
        dv_o[t] = jnp.max(dv[t:t + 1, :])
    input_gradient(1)
    r["gx"][...] = r["o32"][...].astype(BF16)
    store(r["gx"], gx_o)
    arrive("adE")
    r["gab"][...] = mm_tn(r["adf"][...].reshape(2 * th, LANES), r["x"][...])
    store(r["gab"].at[:RANK], ag_o)
    store(r["gab"].at[RANK:], au_o)

    for copy in pending:
        copy.wait_send()
    for copy in stores:
        copy.wait()


def finish_kernel(*refs):
    srcs, dsts, sems = refs[:8], refs[8:16], refs[16]
    copies = [pltpu.make_async_copy(srcs[i], dsts[i], sems.at[i]) for i in range(8)]
    for copy in copies:
        copy.start()
    for copy in copies:
        copy.wait()


def shards(wide, narrow, tokens, cotangent, rewards, group_ids, token_mask, w_gate, w_up, down_w,
           a_gate, a_up, gate_of, up_of, a_down, down_of):
    db, fb = w_gate.shape
    plan = Plan(wide, narrow, db, fb)
    hbm = pl.BlockSpec(memory_space=pltpu.HBM)
    sm = pl.BlockSpec(memory_space=pltpu.SMEM)
    s = jax.ShapeDtypeStruct
    shapes = (
        s((4, db), BF16), s((4,), F32), s((RANK, db), F32), s((RANK, db), F32),
        s((RANK, fb), F32), s((RANK, fb), F32), s((RANK, fb), F32), s((RANK, db), F32),
    )
    mids = pl.pallas_call(
        functools.partial(step_kernel, plan),
        out_shape=shapes,
        in_specs=[hbm, hbm, sm, sm, sm] + [hbm] * 9,
        out_specs=(hbm, sm) + (hbm,) * 6,
        scratch_shapes=plan.shapes,
        compiler_params=pltpu.CompilerParams(
            collective_id=0, has_side_effects=True, vmem_limit_bytes=60 << 20),
        name="policy_step",
    )(tokens, cotangent, rewards, group_ids, token_mask, w_gate, w_up, down_w, a_gate.T, a_up.T,
      gate_of, up_of, a_down.T, down_of)
    outs = pl.pallas_call(
        finish_kernel,
        out_shape=shapes,
        in_specs=[hbm] * 8,
        out_specs=(hbm,) * 8,
        scratch_shapes=[pltpu.SemaphoreType.DMA((8,))],
        compiler_params=pltpu.CompilerParams(vmem_limit_bytes=60 << 20),
        name="finish",
    )(*mids)
    gx, dv, ag, au, gog, uog, gad, dog = outs
    return gx, dv, ag.T, au.T, gog, uog, gad.T, dog


def solution(mesh):
    return jax.shard_map(
        functools.partial(shards, mesh.shape["wide"], mesh.shape["narrow"]),
        mesh=mesh,
        in_specs=(
            P("wide", "narrow"),
            P("wide", "narrow"),
            P("wide"),
            P("wide"),
            P("wide"),
            P("narrow", "wide"),
            P("narrow", "wide"),
            P("wide", "narrow"),
            P("narrow", None),
            P("narrow", None),
            P(None, "wide"),
            P(None, "wide"),
            P("wide", None),
            P(None, "narrow"),
        ),
        out_specs=(
            P("wide", "narrow"),
            P("wide"),
            P("narrow", None),
            P("narrow", None),
            P(None, "wide"),
            P(None, "wide"),
            P("wide", None),
            P(None, "narrow"),
        ),
        check_vma=False,
    )
```

```python
import functools

import jax
import jax.numpy as jnp
from jax import lax
from jax.experimental import pallas as pl
from jax.experimental.pallas import tpu as pltpu
from jax.sharding import PartitionSpec as P

MESH = pl.DeviceIdType.MESH
BF16 = jnp.bfloat16
F32 = jnp.float32
D = 8192
TOKENS = 256
RANK = 64
ADAPTER_SCALE = 2.0
KL_WEIGHT = 0.1
NQ = 8
LANES = 128


def mm(a, b):
    return jnp.dot(a, b, preferred_element_type=F32)


def mm_nt(a, b):
    return lax.dot_general(a, b, (((1,), (1,)), ((), ())), preferred_element_type=F32)


def mm_tn(a, b):
    return lax.dot_general(a, b, (((0,), (0,)), ((), ())), preferred_element_type=F32)


class Plan:
    def __init__(self, wide, narrow, db, fb):
        self.nx = 4 if wide == 64 else 2
        self.ny = wide // (self.nx * 2)
        self.ne = 2 * self.nx
        self.nz = narrow
        self.wide = wide
        self.db, self.fb = db, fb
        self.th = 2 * wide
        self.tz = self.th // narrow
        self.bs = min(16, wide)
        self.yb = self.bs // self.ne
        self.names, self.shapes = [], []
        nx, ny, nz, ne, th, tz = self.nx, self.ny, self.nz, self.ne, self.th, self.tz
        v = self.vmem
        v("wgu", (db, 2 * fb), BF16)
        v("downx", (fb + LANES, db), BF16)
        v("agu", (LANES, db), BF16)
        v("bd", (LANES, 2 * fb), BF16)
        v("adown", (RANK, fb), BF16)
        v("tok", (4, db), BF16)
        v("cot", (4, db), BF16)
        v("t32", (2, 16, LANES), F32)
        v("c32", (2, 16, LANES), F32)
        v("o32", (4, db), F32)
        v("x", (2 * th, db), BF16)
        v("gx", (4, db), BF16)
        v("gab", (LANES, db), F32)
        v("gu", (LANES, 2 * fb), F32)
        v("gad", (RANK, fb), F32)
        v("dog", (RANK, db), F32)
        self.dma("load", 11)
        self.dma("out", 7)
        for h in range(2):
            k = str(h)
            for g in "AD":
                v(g + "g" + k, (ny, nx, 2, 16, LANES), BF16)
                self.rem(g + "y" + k, ny - 1)
                self.rem(g + "x" + k, nx - 1)
                self.rem(g + "c" + k, 1)
            for g in "CF":
                v(g + "r" + k, (ny, nx, 2, 16, LANES), BF16)
                v(g + "rc" + k, (ny, nx, 16, LANES), BF16)
                v(g + "s1" + k, (ny, nx, 16, LANES), BF16)
                v(g + "rx" + k, (nx - 1, ny, 16, LANES), BF16)
                v(g + "s2" + k, (ny, 16, LANES), BF16)
                v(g + "ry" + k, (ny - 1, 16, LANES), BF16)
                self.rem(g + "c" + k, 1)
                self.rem(g + "x" + k, nx - 1)
                self.rem(g + "y" + k, ny - 1)
            for g, width in (("B", 2 * fb + LANES), ("E", fb)):
                v(g + "b" + k, (nz, tz, width), BF16)
                v(g + "r" + k, (nz - 1, tz, width), BF16)
                self.rem(g + "rs" + k, nz - 1)
            for g, width in (("H", fb + LANES), ("K", 3 * fb + LANES), ("E", fb)):
                v(g + "g" + k, (nz, tz, width), BF16)
                self.rem(g + "ag" + k, nz - 1)
            v("go" + k, (th, db), BF16)
            v("ggu" + k, (th, 2 * fb), BF16)
        for g, rows in (("fd", th), ("ad", 2 * th)):
            part = rows // ne
            v(g + "p", (ne, part, LANES), BF16)
            v(g + "re", (ne - 1, part, LANES), BF16)
            v(g + "s", (part, LANES), BF16)
            v(g + "ry", (ny - 1, part, LANES), BF16)
            v(g + "f", (ne, part, LANES), BF16)
            self.rem(g + "e", ne - 1)
            self.rem(g + "y", ny - 1)
            self.rem(g + "E", ne - 1)
        v("Gb", (nz, tz, LANES), BF16)
        v("Gr", (nz - 1, tz, LANES), BF16)
        v("Gg", (nz, tz, LANES), BF16)
        self.rem("Grs", nz - 1)
        self.rem("Gag", nz - 1)
        for name in ("st0", "st1", "dv"):
            v(name, (8, LANES), F32)
        v("ste", (ne - 1, 8, LANES), F32)
        v("sty", (ny - 1, 8, LANES), F32)
        v("dvr", (nz - 1, 8, LANES), F32)
        self.rem("ste_", ne - 1)
        self.rem("sty_", ny - 1)
        self.rem("dv_", nz - 1)

    def vmem(self, name, shape, dtype):
        self.names.append(name)
        self.shapes.append(pltpu.VMEM(shape, dtype))

    def dma(self, name, count):
        self.names.append(name)
        self.shapes.append(pltpu.SemaphoreType.DMA((count,)))

    def rem(self, name, count):
        self.dma(name + ">", count)
        self.dma(name + "<", count)


def step_kernel(plan, *refs):
    (tokens, cotangent, rewards, group_ids, token_mask, w_gate, w_up, down_w, a_gate, a_up,
     gate_of, up_of, a_down, down_of) = refs[:14]
    (gx_o, dv_o, ag_o, au_o, gog_o, uog_o, gad_o, dog_o) = refs[14:22]
    r = dict(zip(plan.names, refs[22:]))
    ny, nx, nz, ne, th, tz, db, fb = (
        plan.ny, plan.nx, plan.nz, plan.ne, plan.th, plan.tz, plan.db, plan.fb)
    w = lax.axis_index("wide")
    z = lax.axis_index("narrow")
    y, x, c = w // ne, (w // 2) % nx, w % 2
    e = w % ne
    other = 1 - c

    ys = [(y + d) % ny for d in range(1, ny)]
    xs = [(x + d) % nx for d in range(1, nx)]
    es = [(e + d) % ne for d in range(1, ne)]
    zs = [(z + d) % nz for d in range(1, nz)]
    dev_y = [(v * ne + e, z) for v in ys]
    dev_x = [(y * ne + v * 2 + c, z) for v in xs]
    dev_e = [(y * ne + v, z) for v in es]
    dev_c = (y * ne + x * 2 + other, z)
    dev_z = [(w, v) for v in zs]
    peers = dev_y + dev_e + dev_z

    barrier = pltpu.get_barrier_semaphore()
    for peer in peers:
        pl.semaphore_signal(barrier, inc=1, device_id=peer, device_id_type=MESH)

    loads = []
    for src, dst in (
        (tokens, r["tok"]), (w_gate, r["wgu"].at[:, :fb]), (w_up, r["wgu"].at[:, fb:]),
        (a_gate, r["agu"].at[:RANK]), (a_up, r["agu"].at[RANK:]),
        (gate_of, r["bd"].at[:RANK, :fb]), (up_of, r["bd"].at[RANK:, fb:]),
        (cotangent, r["cot"]), (down_w, r["downx"].at[:fb]),
        (down_of, r["downx"].at[fb:fb + RANK]), (down_of, r["downx"].at[fb + RANK:]),
    ):
        copy = pltpu.make_async_copy(src, dst, r["load"].at[len(loads)])
        copy.start()
        loads.append(copy)

    pending = []
    flying = {}
    stores = []

    def store(src, dst):
        copy = pltpu.make_async_copy(src, dst, r["out"].at[len(stores)])
        copy.start()
        stores.append(copy)

    def send(name, index, src, dst, device):
        copy = pltpu.make_async_remote_copy(
            src_ref=src, dst_ref=dst, send_sem=r[name + ">"].at[index],
            recv_sem=r[name + "<"].at[index], device_id=device, device_id_type=MESH,
        )
        copy.start()
        pending.append(copy)
        flying.setdefault(name, []).append(copy)

    def arrive(name):
        for copy in flying.pop(name):
            copy.wait_recv()

    def add_up(total, slots, count):
        total = total.astype(F32)
        for i in range(count):
            total += slots[i].astype(F32)
        return total

    def gather_y(g, k):
        buf = r[g + "g" + k]
        for i, device in enumerate(dev_y):
            send(g + "y" + k, i, buf.at[y, x, c], buf.at[y, x, c], device)

    def gather_x(g, k):
        buf = r[g + "g" + k]
        arrive(g + "y" + k)
        for i, device in enumerate(dev_x):
            send(g + "x" + k, i, buf.at[:, x, c], buf.at[:, x, c], device)

    def gather_c(g, k):
        buf = r[g + "g" + k]
        arrive(g + "x" + k)
        send(g + "c" + k, 0, buf.at[:, :, c], buf.at[:, :, c], dev_c)

    def scatter_c(g, k):
        buf = r[g + "r" + k]
        send(g + "c" + k, 0, buf.at[:, :, other], r[g + "rc" + k], dev_c)

    def scatter_x(g, k):
        arrive(g + "c" + k)
        total = r[g + "r" + k][:, :, c].astype(F32) + r[g + "rc" + k][...].astype(F32)
        r[g + "s1" + k][...] = total.astype(BF16)
        for i, device in enumerate(dev_x):
            send(g + "x" + k, i, r[g + "s1" + k].at[:, xs[i]], r[g + "rx" + k].at[i], device)

    def scatter_y(g, k):
        arrive(g + "x" + k)
        total = add_up(r[g + "s1" + k][:, x], r[g + "rx" + k], nx - 1)
        r[g + "s2" + k][...] = total.astype(BF16)
        for i, device in enumerate(dev_y):
            send(g + "y" + k, i, r[g + "s2" + k].at[ys[i]], r[g + "ry" + k].at[i], device)

    def scatter_end(g, k):
        arrive(g + "y" + k)
        return add_up(r[g + "s2" + k][y], r[g + "ry" + k], ny - 1)

    def narrow_sum(g, k):
        for i, device in enumerate(dev_z):
            send(g + "rs" + k, i, r[g + "b" + k].at[zs[i]], r[g + "r" + k].at[i], device)

    def narrow_total(g, k):
        arrive(g + "rs" + k)
        return add_up(r[g + "b" + k][z], r[g + "r" + k], nz - 1)

    def narrow_hand(g, k):
        for i, device in enumerate(dev_z):
            send(g + "ag" + k, i, r[g + "g" + k].at[z], r[g + "g" + k].at[z], device)

    def small_row(g):
        for i, device in enumerate(dev_e):
            send(g + "e", i, r[g + "p"].at[es[i]], r[g + "re"].at[i], device)

    def small_y(g):
        arrive(g + "e")
        r[g + "s"][...] = add_up(r[g + "p"][e], r[g + "re"], ne - 1).astype(BF16)
        for i, device in enumerate(dev_y):
            send(g + "y", i, r[g + "s"], r[g + "ry"].at[i], device)

    def small_hand(g):
        arrive(g + "y")
        r[g + "f"][e] = add_up(r[g + "s"][...], r[g + "ry"], ny - 1).astype(BF16)
        for i, device in enumerate(dev_e):
            send(g + "E", i, r[g + "f"].at[e], r[g + "f"].at[e], device)

    rows = plan.bs * 16
    row = lax.broadcasted_iota(jnp.int32, (rows, rows), 0)
    col = lax.broadcasted_iota(jnp.int32, (rows, rows), 1)

    def by_block(v):
        return ((v >> 1) & 7) * (2 * plan.bs) + (v >> 4) * 2 + (v & 1)

    to_tokens = (row == by_block(col)).astype(F32).astype(BF16)
    to_shards = (col == by_block(row)).astype(F32).astype(BF16)

    def unpack(g, k, out, base):
        for b in range(plan.wide // plan.bs):
            block = r[g + "g" + k][plan.yb * b:plan.yb * (b + 1)].reshape(rows, LANES)
            turned = mm(to_tokens, block).astype(BF16)
            n = 2 * plan.bs
            for q in range(NQ):
                out[base + n * b:base + n * (b + 1), LANES * q:LANES * (q + 1)] = (
                    turned[n * q:n * (q + 1)])

    def pack(value, g, k):
        for b in range(plan.wide // plan.bs):
            n = 2 * plan.bs
            block = jnp.concatenate(
                [value[n * b:n * (b + 1), LANES * q:LANES * (q + 1)] for q in range(NQ)], axis=0)
            turned = mm(to_shards, block).astype(BF16)
            r[g + "r" + k][plan.yb * b:plan.yb * (b + 1)] = turned.reshape(
                plan.yb, nx, 2, 16, LANES)

    loads[0].wait()
    tok = r["tok"][...].astype(F32)
    for h in range(2):
        for q in range(NQ):
            r["t32"][h, 2 * q:2 * q + 2, :] = tok[2 * h:2 * h + 2, LANES * q:LANES * (q + 1)]
        r["Ag" + str(h)][y, x, c] = r["t32"][h].astype(BF16)

    lane = lax.broadcasted_iota(jnp.int32, (1, LANES), 1)
    mask = [token_mask[t].astype(F32) for t in range(4)]
    reward = [rewards[t] for t in range(4)]
    ids = [group_ids[t] for t in range(4)]
    reward_row = jnp.zeros((1, LANES), F32)
    count_row = jnp.zeros((1, LANES), F32)
    for t in range(4):
        reward_row += jnp.where(lane == ids[t], mask[t] * reward[t], 0.0)
        count_row += jnp.where(lane == ids[t], mask[t], 0.0)
    row8 = lax.broadcasted_iota(jnp.int32, (8, LANES), 0)
    r["st0"][...] = jnp.where(row8 == 0, reward_row, jnp.where(row8 == 1, count_row, 0.0))

    pl.semaphore_wait(barrier, len(peers))
    gather_y("A", "0")
    gather_y("A", "1")
    for i, device in enumerate(dev_e):
        send("ste_", i, r["st0"], r["ste"].at[i], device)
    loads[7].wait()
    cot = r["cot"][...].astype(F32)
    for h in range(2):
        for q in range(NQ):
            r["c32"][h, 2 * q:2 * q + 2, :] = cot[2 * h:2 * h + 2, LANES * q:LANES * (q + 1)]
    r["bd"][:RANK, fb:] = jnp.zeros((RANK, fb), BF16)
    r["bd"][RANK:, :fb] = jnp.zeros((RANK, fb), BF16)
    loads[0] = pltpu.make_async_copy(a_down, r["adown"], r["load"].at[0])
    loads[0].start()
    gather_x("A", "0")
    gather_x("A", "1")

    arrive("ste_")
    r["st1"][...] = add_up(r["st0"][...], r["ste"], ne - 1)
    for i, device in enumerate(dev_y):
        send("sty_", i, r["st1"], r["sty"].at[i], device)
    for i in (1, 2, 3, 4, 5, 6):
        loads[i].wait()
    gather_c("A", "0")
    gather_c("A", "1")

    def project(h):
        k = str(h)
        arrive("Ac" + k)
        unpack("A", k, r["x"], h * th)
        xv = r["x"][h * th:(h + 1) * th]
        r["Bb" + k][:, :, 2 * fb:] = (
            mm_nt(xv, r["agu"][...]).astype(BF16).reshape(nz, tz, LANES))
        r["Bb" + k][:, :, :2 * fb] = (
            mm(xv, r["wgu"][...]).astype(BF16).reshape(nz, tz, 2 * fb))
        narrow_sum("B", k)

    project(0)
    project(1)

    arrive("sty_")
    stats = add_up(r["st1"][...], r["sty"], ny - 1)
    group_count = stats[1:2]
    group_mean = stats[0:1] / jnp.maximum(group_count, 1.0)
    all_count = jnp.sum(group_count, axis=1, keepdims=True)
    scale_of = TOKENS / jnp.maximum(all_count, 1.0)
    advantage, token_scale = [], []
    for t in range(4):
        mean_t = jnp.sum(jnp.where(lane == ids[t], group_mean, 0.0), axis=1, keepdims=True)
        advantage.append(reward[t] - mean_t)
        token_scale.append(mask[t] * scale_of)
    loads[0].wait()

    def hidden(h):
        k = str(h)
        total = narrow_total("B", k)
        factors = total[:, 2 * fb:].astype(BF16)
        adapt = ADAPTER_SCALE * mm(factors, r["bd"][...])
        gate_base = total[:, :fb]
        up_base = total[:, fb:2 * fb]
        gate = gate_base + adapt[:, :fb]
        up = up_base + adapt[:, fb:]
        sig = jax.nn.sigmoid(gate)
        silu = gate * sig
        slope = sig * (1.0 + gate * (1.0 - sig))
        full = silu * up
        hp = full.astype(BF16)
        hd = (full - gate_base * jax.nn.sigmoid(gate_base) * up_base).astype(BF16)
        fd = ADAPTER_SCALE * mm_nt(hp, r["adown"][...])
        none = jnp.zeros_like(fd)
        fd = jnp.concatenate([none, fd] if h else [fd, none], axis=1)
        r["Hg" + k][z, :, :fb] = hd
        r["Hg" + k][z, :, fb:] = fd.astype(BF16)
        narrow_hand("H", k)
        r["Kg" + k][z, :, :fb] = (up * slope).astype(BF16)
        r["Kg" + k][z, :, fb:2 * fb] = silu.astype(BF16)
        r["Kg" + k][z, :, 2 * fb:3 * fb] = hp
        r["Kg" + k][z, :, 3 * fb:] = factors

    hidden(0)
    hidden(1)
    narrow_hand("K", "0")
    narrow_hand("K", "1")
    for i in (8, 9, 10):
        loads[i].wait()

    def outward(h):
        k = str(h)
        arrive("Hag" + k)
        both = r["Hg" + k][...].reshape(th, fb + LANES)
        pack(mm(both, r["downx"][...]).astype(BF16), "C", k)
        scatter_c("C", k)
        return both[:, fb:].astype(F32)

    row16 = lax.broadcasted_iota(jnp.int32, (16, 1), 0)
    even = (row16 & 1) == 0
    div = []

    def gradient(h):
        k = str(h)
        od = scatter_end("C", k)
        adv = jnp.where(even, advantage[2 * h], advantage[2 * h + 1])
        scl = jnp.where(even, token_scale[2 * h], token_scale[2 * h + 1])
        grad = scl * (KL_WEIGHT * od - adv * r["c32"][h])
        r["Dg" + k][y, x, c] = grad.astype(BF16)
        gather_y("D", k)
        square = od * od
        for t in range(2):
            picked = jnp.where(((row16 & 1) == t), square, 0.0)
            div.append(jnp.sum(jnp.sum(picked, axis=1, keepdims=True), axis=0, keepdims=True))

    fd0 = outward(0)
    scatter_x("C", "0")
    fd1 = outward(1)
    r["fdp"][...] = (fd0 + fd1).astype(BF16).reshape(ne, th // ne, LANES)
    small_row("fd")
    scatter_y("C", "0")
    scatter_x("C", "1")
    gradient(0)
    scatter_y("C", "1")
    small_y("fd")
    gather_x("D", "0")
    gradient(1)
    dv = jnp.zeros((8, LANES), F32)
    for t in range(4):
        dv += jnp.where(row8 == t, div[t], 0.0)
    r["dv"][...] = dv * (0.5 / D)
    for i, device in enumerate(dev_z):
        send("dv_", i, r["dv"], r["dvr"].at[i], device)
    gather_c("D", "0")
    gather_x("D", "1")
    small_hand("fd")

    def inward(h):
        k = str(h)
        arrive("Dc" + k)
        unpack("D", k, r["go" + k], 0)
        both = mm_nt(r["go" + k][...], r["downx"][...])
        gf = ADAPTER_SCALE * both[:, fb:]
        gh = both[:, :fb] + mm(gf[:, :RANK].astype(BF16), r["adown"][...])
        r["Eb" + k][...] = gh.astype(BF16).reshape(nz, tz, fb)
        narrow_sum("E", k)
        return gf

    gf0 = inward(0)
    gather_c("D", "1")
    gf1 = inward(1)
    r["Gb"][...] = jnp.where(lane < RANK, gf0, gf1).astype(BF16).reshape(nz, tz, LANES)
    for i, device in enumerate(dev_z):
        send("Grs", i, r["Gb"].at[zs[i]], r["Gr"].at[i], device)
    r["Eg0"][z] = narrow_total("E", "0").astype(BF16)
    narrow_hand("E", "0")
    arrive("fdE")
    fdf = r["fdf"][...].reshape(th, LANES)
    r["dog"][...] = mm_tn(fdf, r["go0"][...])[:RANK] + mm_tn(fdf, r["go1"][...])[RANK:]
    store(r["dog"], dog_o)
    r["Eg1"][z] = narrow_total("E", "1").astype(BF16)
    narrow_hand("E", "1")
    arrive("Grs")
    r["Gg"][z] = add_up(r["Gb"][z], r["Gr"], nz - 1).astype(BF16)
    for i, device in enumerate(dev_z):
        send("Gag", i, r["Gg"].at[z], r["Gg"].at[z], device)
    arrive("Kag0")
    arrive("Kag1")

    def back(h):
        k = str(h)
        arrive("Eag" + k)
        gh = r["Eg" + k][...].reshape(th, fb).astype(F32)
        kept = r["Kg" + k][...].reshape(th, 3 * fb + LANES)
        r["ggu" + k][:, :fb] = (gh * kept[:, :fb].astype(F32)).astype(BF16)
        r["ggu" + k][:, fb:] = (gh * kept[:, fb:2 * fb].astype(F32)).astype(BF16)
        ggu = r["ggu" + k][...]
        ad = (ADAPTER_SCALE * mm_nt(ggu, r["bd"][...])).astype(BF16)
        r["adp"][h * nx:(h + 1) * nx] = ad.reshape(nx, 2 * th // ne, LANES)
        if h == 1:
            small_row("ad")
        gx = mm_nt(ggu, r["wgu"][...]) + mm(ad, r["agu"][...])
        pack(gx.astype(BF16), "F", k)
        scatter_c("F", k)

    back(0)
    scatter_x("F", "0")
    back(1)
    scatter_y("F", "0")
    scatter_x("F", "1")
    small_y("ad")
    gu = jnp.zeros((LANES, 2 * fb), F32)
    for h in range(2):
        k = str(h)
        factors = r["Kg" + k][:, :, 3 * fb:].reshape(th, LANES)
        gu += mm_tn(factors, r["ggu" + k][...])
    r["gu"][...] = ADAPTER_SCALE * gu
    store(r["gu"].at[:RANK, :fb], gog_o)
    store(r["gu"].at[RANK:, fb:], uog_o)

    def input_gradient(h):
        gx = scatter_end("F", str(h))
        for q in range(NQ):
            r["o32"][2 * h:2 * h + 2, LANES * q:LANES * (q + 1)] = gx[2 * q:2 * q + 2]

    scatter_y("F", "1")
    small_hand("ad")
    input_gradient(0)
    arrive("Gag")
    gff = r["Gg"][...].reshape(th, LANES)
    parts = [mm_tn(gff, r["Kg" + k][:, :, 2 * fb:3 * fb].reshape(th, fb)) for k in "01"]
    r["gad"][...] = parts[0][:RANK] + parts[1][RANK:]
    store(r["gad"], gad_o)
    arrive("dv_")
    dv = add_up(r["dv"][...], r["dvr"], nz - 1)
    for t in range(4):
        dv_o[t] = jnp.max(dv[t:t + 1, :])
    input_gradient(1)
    r["gx"][...] = r["o32"][...].astype(BF16)
    store(r["gx"], gx_o)
    arrive("adE")
    r["gab"][...] = mm_tn(r["adf"][...].reshape(2 * th, LANES), r["x"][...])
    store(r["gab"].at[:RANK], ag_o)
    store(r["gab"].at[RANK:], au_o)

    for copy in pending:
        copy.wait_send()
    for copy in stores:
        copy.wait()


def finish_kernel(*refs):
    srcs, dsts, held, sems = refs[:8], refs[8:16], refs[16:24], refs[24]
    ins = [pltpu.make_async_copy(srcs[i], held[i], sems.at[i]) for i in range(8)]
    outs = [pltpu.make_async_copy(held[i], dsts[i], sems.at[8 + i]) for i in range(8)]
    for copy in ins:
        copy.start()
    for i in range(8):
        ins[i].wait()
        outs[i].start()
    for copy in outs:
        copy.wait()


def shards(wide, narrow, tokens, cotangent, rewards, group_ids, token_mask, w_gate, w_up, down_w,
           a_gate, a_up, gate_of, up_of, a_down, down_of):
    db, fb = w_gate.shape
    plan = Plan(wide, narrow, db, fb)
    hbm = pl.BlockSpec(memory_space=pltpu.HBM)
    sm = pl.BlockSpec(memory_space=pltpu.SMEM)
    s = jax.ShapeDtypeStruct
    shapes = (
        s((4, db), BF16), s((4,), F32), s((RANK, db), F32), s((RANK, db), F32),
        s((RANK, fb), F32), s((RANK, fb), F32), s((RANK, fb), F32), s((RANK, db), F32),
    )
    mids = pl.pallas_call(
        functools.partial(step_kernel, plan),
        out_shape=shapes,
        in_specs=[hbm, hbm, sm, sm, sm] + [hbm] * 9,
        out_specs=(hbm, sm) + (hbm,) * 6,
        scratch_shapes=plan.shapes,
        compiler_params=pltpu.CompilerParams(
            collective_id=0, has_side_effects=True, vmem_limit_bytes=60 << 20),
        name="policy_step",
    )(tokens, cotangent, rewards, group_ids, token_mask, w_gate, w_up, down_w, a_gate.T, a_up.T,
      gate_of, up_of, a_down.T, down_of)
    outs = pl.pallas_call(
        finish_kernel,
        out_shape=shapes,
        in_specs=[hbm] * 8,
        out_specs=(hbm,) * 8,
        scratch_shapes=[pltpu.VMEM(v.shape, v.dtype) for v in shapes]
        + [pltpu.SemaphoreType.DMA((16,))],
        compiler_params=pltpu.CompilerParams(vmem_limit_bytes=60 << 20),
        name="finish",
    )(*mids)
    gx, dv, ag, au, gog, uog, gad, dog = outs
    return gx, dv, ag.T, au.T, gog, uog, gad.T, dog


def solution(mesh):
    return jax.shard_map(
        functools.partial(shards, mesh.shape["wide"], mesh.shape["narrow"]),
        mesh=mesh,
        in_specs=(
            P("wide", "narrow"),
            P("wide", "narrow"),
            P("wide"),
            P("wide"),
            P("wide"),
            P("narrow", "wide"),
            P("narrow", "wide"),
            P("wide", "narrow"),
            P("narrow", None),
            P("narrow", None),
            P(None, "wide"),
            P(None, "wide"),
            P("wide", None),
            P(None, "narrow"),
        ),
        out_specs=(
            P("wide", "narrow"),
            P("wide"),
            P("narrow", None),
            P("narrow", None),
            P(None, "wide"),
            P(None, "wide"),
            P("wide", None),
            P(None, "narrow"),
        ),
        check_vma=False,
    )
```

```python
import functools

import jax
import jax.numpy as jnp
from jax import lax
from jax.experimental import pallas as pl
from jax.experimental.pallas import tpu as pltpu
from jax.sharding import PartitionSpec as P

MESH = pl.DeviceIdType.MESH
BF16 = jnp.bfloat16
F32 = jnp.float32
D = 8192
TOKENS = 256
RANK = 64
ADAPTER_SCALE = 2.0
KL_WEIGHT = 0.1
NQ = 8
LANES = 128


def mm(a, b):
    return jnp.dot(a, b, preferred_element_type=F32)


def mm_nt(a, b):
    return lax.dot_general(a, b, (((1,), (1,)), ((), ())), preferred_element_type=F32)


def mm_tn(a, b):
    return lax.dot_general(a, b, (((0,), (0,)), ((), ())), preferred_element_type=F32)


class Plan:
    def __init__(self, wide, narrow, db, fb):
        self.nx = 4 if wide == 64 else 2
        self.ny = wide // (self.nx * 2)
        self.ne = 2 * self.nx
        self.nz = narrow
        self.wide = wide
        self.db, self.fb = db, fb
        self.th = 2 * wide
        self.tz = self.th // narrow
        self.bs = min(16, wide)
        self.yb = self.bs // self.ne
        self.names, self.shapes = [], []
        nx, ny, nz, ne, th, tz = self.nx, self.ny, self.nz, self.ne, self.th, self.tz
        v = self.vmem
        v("wgu", (db, 2 * fb), BF16)
        v("downx", (fb + LANES, db), BF16)
        v("agu", (LANES, db), BF16)
        v("bd", (LANES, 2 * fb), BF16)
        v("adown", (RANK, fb), BF16)
        v("tok", (4, db), BF16)
        v("cot", (4, db), BF16)
        v("t32", (2, 16, LANES), F32)
        v("c32", (2, 16, LANES), F32)
        v("o32", (4, db), F32)
        v("x", (2 * th, db), BF16)
        v("gx", (4, db), BF16)
        v("gab", (LANES, db), F32)
        v("gu", (LANES, 2 * fb), F32)
        v("gad", (RANK, fb), F32)
        v("dog", (RANK, db), F32)
        self.dma("load", 12)
        self.dma("out", 7)
        for h in range(2):
            k = str(h)
            for g in "AD":
                v(g + "g" + k, (ny, nx, 2, 16, LANES), BF16)
                self.rem(g + "y" + k, ny - 1)
                self.rem(g + "x" + k, nx - 1)
                self.rem(g + "c" + k, 1)
            for g in "CF":
                v(g + "r" + k, (ny, nx, 2, 16, LANES), BF16)
                v(g + "rc" + k, (ny, nx, 16, LANES), BF16)
                v(g + "s1" + k, (ny, nx, 16, LANES), BF16)
                v(g + "rx" + k, (nx - 1, ny, 16, LANES), BF16)
                v(g + "s2" + k, (ny, 16, LANES), BF16)
                v(g + "ry" + k, (ny - 1, 16, LANES), BF16)
                self.rem(g + "c" + k, 1)
                self.rem(g + "x" + k, nx - 1)
                self.rem(g + "y" + k, ny - 1)
            for g, width in (("B", 2 * fb + LANES), ("E", fb)):
                v(g + "b" + k, (nz, tz, width), BF16)
                v(g + "r" + k, (nz - 1, tz, width), BF16)
                self.rem(g + "rs" + k, nz - 1)
            for g, width in (("H", fb + LANES), ("K", 2 * fb + LANES), ("E", fb)):
                v(g + "g" + k, (nz, tz, width), BF16)
                self.rem(g + "ag" + k, nz - 1)
            v("hp" + k, (tz, fb), BF16)
            v("go" + k, (th, db), BF16)
            v("ggu" + k, (th, 2 * fb), BF16)
        part = th // ne
        v("fdp", (ne, part, LANES), BF16)
        v("fdre", (ne - 1, part, LANES), BF16)
        v("fds", (part, LANES), BF16)
        v("fdry", (ny - 1, part, LANES), BF16)
        v("fdf", (ne, part, LANES), BF16)
        self.rem("fde", ne - 1)
        self.rem("fdy", ny - 1)
        self.rem("fdE", ne - 1)
        v("adp", (2, tz, LANES), BF16)
        v("adre", (ne - 1, 2, tz, LANES), BF16)
        v("ads", (2, tz, LANES), BF16)
        v("adry", (ny - 1, 2, tz, LANES), BF16)
        v("adf", (2, nz, tz, LANES), BF16)
        self.rem("ade", ne - 1)
        self.rem("ady", ny - 1)
        self.rem("adz", nz - 1)
        v("Gb", (nz, tz, LANES), BF16)
        v("Gr", (nz - 1, tz, LANES), BF16)
        self.rem("Grs", nz - 1)
        self.rb, self.cb = 2 * RANK // nz, fb // 2
        v("Mb", (nz, self.rb, self.cb), BF16)
        v("Mr", (nz - 1, self.rb, self.cb), BF16)
        v("Mg", (nz, self.rb, self.cb), F32)
        self.rem("Mrs", nz - 1)
        self.rem("Mag", nz - 1)
        for name in ("st0", "st1", "dv"):
            v(name, (8, LANES), F32)
        v("ste", (ne - 1, 8, LANES), F32)
        v("sty", (ny - 1, 8, LANES), F32)
        v("dvr", (nz - 1, 8, LANES), F32)
        self.rem("ste_", ne - 1)
        self.rem("sty_", ny - 1)
        self.rem("dv_", nz - 1)

    def vmem(self, name, shape, dtype):
        self.names.append(name)
        self.shapes.append(pltpu.VMEM(shape, dtype))

    def dma(self, name, count):
        self.names.append(name)
        self.shapes.append(pltpu.SemaphoreType.DMA((count,)))

    def rem(self, name, count):
        self.dma(name + ">", count)
        self.dma(name + "<", count)


def step_kernel(plan, *refs):
    (tokens, cotangent, rewards, group_ids, token_mask, w_gate, w_up, down_w, a_gate, a_up,
     gate_of, up_of, a_down, down_of) = refs[:14]
    (gx_o, dv_o, ag_o, au_o, gog_o, uog_o, gad_o, dog_o) = refs[14:22]
    r = dict(zip(plan.names, refs[22:]))
    ny, nx, nz, ne, th, tz, db, fb = (
        plan.ny, plan.nx, plan.nz, plan.ne, plan.th, plan.tz, plan.db, plan.fb)
    w = lax.axis_index("wide")
    z = lax.axis_index("narrow")
    y, x, c = w // ne, (w // 2) % nx, w % 2
    e = w % ne
    other = 1 - c

    def far_first(n):
        return sorted(range(1, n), key=lambda d: -min(d, n - d))

    ys = [(y + d) % ny for d in far_first(ny)]
    xs = [(x + d) % nx for d in far_first(nx)]
    es = [((x + d) % nx) * 2 + v for d in far_first(nx) for v in (c, other)] + [x * 2 + other]
    zs = [(z + d) % nz for d in far_first(nz)]
    dev_y = [(v * ne + e, z) for v in ys]
    dev_x = [(y * ne + v * 2 + c, z) for v in xs]
    dev_e = [(y * ne + v, z) for v in es]
    dev_c = (y * ne + x * 2 + other, z)
    dev_z = [(w, v) for v in zs]
    peers = dev_y + dev_e + dev_z

    barrier = pltpu.get_barrier_semaphore()
    for peer in peers:
        pl.semaphore_signal(barrier, inc=1, device_id=peer, device_id_type=MESH)

    loads = []

    def load(src, dst):
        copy = pltpu.make_async_copy(src, dst, r["load"].at[len(loads)])
        copy.start()
        loads.append(copy)

    load(tokens, r["tok"])
    load(cotangent, r["cot"])

    pending = []
    flying = {}
    stores = []

    def store(src, dst):
        copy = pltpu.make_async_copy(src, dst, r["out"].at[len(stores)])
        copy.start()
        stores.append(copy)

    def send(name, index, src, dst, device):
        copy = pltpu.make_async_remote_copy(
            src_ref=src, dst_ref=dst, send_sem=r[name + ">"].at[index],
            recv_sem=r[name + "<"].at[index], device_id=device, device_id_type=MESH,
        )
        copy.start()
        pending.append(copy)
        flying.setdefault(name, []).append(copy)

    def settle():
        for copy in pending:
            copy.wait_send()
        pending.clear()

    def arrive(name):
        for copy in flying.pop(name):
            copy.wait_recv()

    def add_up(total, slots, count):
        total = total.astype(F32)
        for i in range(count):
            total += slots[i].astype(F32)
        return total

    def gather_y(g, k):
        buf = r[g + "g" + k]
        for i, device in enumerate(dev_y):
            send(g + "y" + k, i, buf.at[y, x, c], buf.at[y, x, c], device)

    def gather_x(g, k):
        buf = r[g + "g" + k]
        arrive(g + "y" + k)
        for i, device in enumerate(dev_x):
            send(g + "x" + k, i, buf.at[:, x, c], buf.at[:, x, c], device)

    def gather_c(g, k):
        buf = r[g + "g" + k]
        arrive(g + "x" + k)
        send(g + "c" + k, 0, buf.at[:, :, c], buf.at[:, :, c], dev_c)

    def scatter_c(g, k):
        buf = r[g + "r" + k]
        send(g + "c" + k, 0, buf.at[:, :, other], r[g + "rc" + k], dev_c)

    def scatter_x(g, k):
        arrive(g + "c" + k)
        total = r[g + "r" + k][:, :, c].astype(F32) + r[g + "rc" + k][...].astype(F32)
        r[g + "s1" + k][...] = total.astype(BF16)
        for i, device in enumerate(dev_x):
            send(g + "x" + k, i, r[g + "s1" + k].at[:, xs[i]], r[g + "rx" + k].at[i], device)

    def scatter_y(g, k):
        arrive(g + "x" + k)
        total = add_up(r[g + "s1" + k][:, x], r[g + "rx" + k], nx - 1)
        r[g + "s2" + k][...] = total.astype(BF16)
        for i, device in enumerate(dev_y):
            send(g + "y" + k, i, r[g + "s2" + k].at[ys[i]], r[g + "ry" + k].at[i], device)

    def scatter_end(g, k):
        arrive(g + "y" + k)
        return add_up(r[g + "s2" + k][y], r[g + "ry" + k], ny - 1)

    def narrow_sum(g, k):
        for i, device in enumerate(dev_z):
            send(g + "rs" + k, i, r[g + "b" + k].at[zs[i]], r[g + "r" + k].at[i], device)

    def narrow_total(g, k):
        arrive(g + "rs" + k)
        return add_up(r[g + "b" + k][z], r[g + "r" + k], nz - 1)

    def narrow_hand(g, k):
        for i, device in enumerate(dev_z):
            send(g + "ag" + k, i, r[g + "g" + k].at[z], r[g + "g" + k].at[z], device)

    def small_row(g):
        for i, device in enumerate(dev_e):
            send(g + "e", i, r[g + "p"].at[es[i]], r[g + "re"].at[i], device)

    def small_y(g):
        arrive(g + "e")
        r[g + "s"][...] = add_up(r[g + "p"][e], r[g + "re"], ne - 1).astype(BF16)
        for i, device in enumerate(dev_y):
            send(g + "y", i, r[g + "s"], r[g + "ry"].at[i], device)

    def small_hand(g):
        arrive(g + "y")
        r[g + "f"][e] = add_up(r[g + "s"][...], r[g + "ry"], ny - 1).astype(BF16)
        for i, device in enumerate(dev_e):
            send(g + "E", i, r[g + "f"].at[e], r[g + "f"].at[e], device)

    loads[0].wait()
    tok = r["tok"][...].astype(F32)
    for h in range(2):
        for q in range(NQ):
            r["t32"][h, 2 * q:2 * q + 2, :] = tok[2 * h:2 * h + 2, LANES * q:LANES * (q + 1)]
        r["Ag" + str(h)][y, x, c] = r["t32"][h].astype(BF16)

    lane = lax.broadcasted_iota(jnp.int32, (1, LANES), 1)
    mask = [token_mask[t].astype(F32) for t in range(4)]
    reward = [rewards[t] for t in range(4)]
    ids = [group_ids[t] for t in range(4)]
    reward_row = jnp.zeros((1, LANES), F32)
    count_row = jnp.zeros((1, LANES), F32)
    for t in range(4):
        reward_row += jnp.where(lane == ids[t], mask[t] * reward[t], 0.0)
        count_row += jnp.where(lane == ids[t], mask[t], 0.0)
    row8 = lax.broadcasted_iota(jnp.int32, (8, LANES), 0)
    r["st0"][...] = jnp.where(row8 == 0, reward_row, jnp.where(row8 == 1, count_row, 0.0))

    pl.semaphore_wait(barrier, len(peers))
    gather_y("A", "0")
    gather_y("A", "1")
    for i, device in enumerate(dev_e):
        send("ste_", i, r["st0"], r["ste"].at[i], device)
    load(w_gate, r["wgu"].at[:, :fb])
    load(w_up, r["wgu"].at[:, fb:])
    load(a_gate, r["agu"].at[:RANK])
    load(a_up, r["agu"].at[RANK:])
    load(gate_of, r["bd"].at[:RANK, :fb])
    load(up_of, r["bd"].at[RANK:, fb:])
    load(down_w, r["downx"].at[:fb])
    load(down_of, r["downx"].at[fb:fb + RANK])
    load(down_of, r["downx"].at[fb + RANK:])
    load(a_down, r["adown"])

    rows = plan.bs * 16
    row = lax.broadcasted_iota(jnp.int32, (rows, rows), 0)
    col = lax.broadcasted_iota(jnp.int32, (rows, rows), 1)

    def by_block(v):
        return ((v >> 1) & 7) * (2 * plan.bs) + (v >> 4) * 2 + (v & 1)

    to_tokens = (row == by_block(col)).astype(F32).astype(BF16)
    to_shards = (col == by_block(row)).astype(F32).astype(BF16)

    def unpack(g, k, out, base):
        for b in range(plan.wide // plan.bs):
            block = r[g + "g" + k][plan.yb * b:plan.yb * (b + 1)].reshape(rows, LANES)
            turned = mm(to_tokens, block).astype(BF16)
            n = 2 * plan.bs
            for q in range(NQ):
                out[base + n * b:base + n * (b + 1), LANES * q:LANES * (q + 1)] = (
                    turned[n * q:n * (q + 1)])

    def pack(value, g, k):
        for b in range(plan.wide // plan.bs):
            n = 2 * plan.bs
            block = jnp.concatenate(
                [value[n * b:n * (b + 1), LANES * q:LANES * (q + 1)] for q in range(NQ)], axis=0)
            turned = mm(to_shards, block).astype(BF16)
            r[g + "r" + k][plan.yb * b:plan.yb * (b + 1)] = turned.reshape(
                plan.yb, nx, 2, 16, LANES)

    loads[1].wait()
    cot = r["cot"][...].astype(F32)
    for h in range(2):
        for q in range(NQ):
            r["c32"][h, 2 * q:2 * q + 2, :] = cot[2 * h:2 * h + 2, LANES * q:LANES * (q + 1)]
    r["bd"][:RANK, fb:] = jnp.zeros((RANK, fb), BF16)
    r["bd"][RANK:, :fb] = jnp.zeros((RANK, fb), BF16)
    gather_x("A", "0")
    gather_x("A", "1")

    arrive("ste_")
    r["st1"][...] = add_up(r["st0"][...], r["ste"], ne - 1)
    for i, device in enumerate(dev_y):
        send("sty_", i, r["st1"], r["sty"].at[i], device)
    for i in range(2, 8):
        loads[i].wait()
    gather_c("A", "0")
    gather_c("A", "1")

    def project(h):
        k = str(h)
        arrive("Ac" + k)
        unpack("A", k, r["x"], h * th)
        xv = r["x"][h * th:(h + 1) * th]
        r["Bb" + k][:, :, 2 * fb:] = (
            mm_nt(xv, r["agu"][...]).astype(BF16).reshape(nz, tz, LANES))
        r["Bb" + k][:, :, :2 * fb] = (
            mm(xv, r["wgu"][...]).astype(BF16).reshape(nz, tz, 2 * fb))
        narrow_sum("B", k)

    project(0)
    project(1)

    arrive("sty_")
    stats = add_up(r["st1"][...], r["sty"], ny - 1)
    group_count = stats[1:2]
    group_mean = stats[0:1] / jnp.maximum(group_count, 1.0)
    all_count = jnp.sum(group_count, axis=1, keepdims=True)
    scale_of = TOKENS / jnp.maximum(all_count, 1.0)
    advantage, token_scale = [], []
    for t in range(4):
        mean_t = jnp.sum(jnp.where(lane == ids[t], group_mean, 0.0), axis=1, keepdims=True)
        advantage.append(reward[t] - mean_t)
        token_scale.append(mask[t] * scale_of)
    loads[11].wait()

    def hidden(h):
        k = str(h)
        total = narrow_total("B", k)
        factors = total[:, 2 * fb:].astype(BF16)
        adapt = ADAPTER_SCALE * mm(factors, r["bd"][...])
        gate_base = total[:, :fb]
        up_base = total[:, fb:2 * fb]
        gate = gate_base + adapt[:, :fb]
        up = up_base + adapt[:, fb:]
        sig = jax.nn.sigmoid(gate)
        silu = gate * sig
        slope = sig * (1.0 + gate * (1.0 - sig))
        full = silu * up
        hp = full.astype(BF16)
        hd = (full - gate_base * jax.nn.sigmoid(gate_base) * up_base).astype(BF16)
        fd = ADAPTER_SCALE * mm_nt(hp, r["adown"][...])
        none = jnp.zeros_like(fd)
        fd = jnp.concatenate([none, fd] if h else [fd, none], axis=1)
        r["Hg" + k][z, :, :fb] = hd
        r["Hg" + k][z, :, fb:] = fd.astype(BF16)
        narrow_hand("H", k)
        r["Kg" + k][z, :, :fb] = (up * slope).astype(BF16)
        r["Kg" + k][z, :, fb:2 * fb] = silu.astype(BF16)
        r["Kg" + k][z, :, 2 * fb:] = factors
        r["hp" + k][...] = hp

    hidden(0)
    hidden(1)
    for i in range(8, 11):
        loads[i].wait()

    def outward(h):
        k = str(h)
        arrive("Hag" + k)
        both = r["Hg" + k][...].reshape(th, fb + LANES)
        pack(mm(both, r["downx"][...]).astype(BF16), "C", k)
        scatter_c("C", k)
        return both[:, fb:].astype(F32)

    row16 = lax.broadcasted_iota(jnp.int32, (16, 1), 0)
    even = (row16 & 1) == 0
    div = []

    def gradient(h):
        k = str(h)
        od = scatter_end("C", k)
        adv = jnp.where(even, advantage[2 * h], advantage[2 * h + 1])
        scl = jnp.where(even, token_scale[2 * h], token_scale[2 * h + 1])
        grad = scl * (KL_WEIGHT * od - adv * r["c32"][h])
        r["Dg" + k][y, x, c] = grad.astype(BF16)
        gather_y("D", k)
        square = od * od
        for t in range(2):
            picked = jnp.where(((row16 & 1) == t), square, 0.0)
            div.append(jnp.sum(jnp.sum(picked, axis=1, keepdims=True), axis=0, keepdims=True))

    fd0 = outward(0)
    scatter_x("C", "0")
    fd1 = outward(1)
    settle()
    narrow_hand("K", "0")
    r["fdp"][...] = (fd0 + fd1).astype(BF16).reshape(ne, th // ne, LANES)
    small_row("fd")
    scatter_y("C", "0")
    scatter_x("C", "1")
    gradient(0)
    narrow_hand("K", "1")
    scatter_y("C", "1")
    small_y("fd")
    gather_x("D", "0")
    gradient(1)
    dv = jnp.zeros((8, LANES), F32)
    for t in range(4):
        dv += jnp.where(row8 == t, div[t], 0.0)
    r["dv"][...] = dv * (0.5 / D)
    for i, device in enumerate(dev_z):
        send("dv_", i, r["dv"], r["dvr"].at[i], device)
    gather_c("D", "0")
    gather_x("D", "1")
    small_hand("fd")
    settle()

    def inward(h):
        k = str(h)
        arrive("Dc" + k)
        unpack("D", k, r["go" + k], 0)
        both = mm_nt(r["go" + k][...], r["downx"][...])
        gf = ADAPTER_SCALE * both[:, fb:]
        gh = both[:, :fb] + mm(gf[:, :RANK].astype(BF16), r["adown"][...])
        r["Eb" + k][...] = gh.astype(BF16).reshape(nz, tz, fb)
        narrow_sum("E", k)
        return gf

    gf0 = inward(0)
    gather_c("D", "1")
    gf1 = inward(1)
    r["Gb"][...] = jnp.where(lane < RANK, gf0, gf1).astype(BF16).reshape(nz, tz, LANES)
    for i, device in enumerate(dev_z):
        send("Grs", i, r["Gb"].at[zs[i]], r["Gr"].at[i], device)
    def adapters(h):
        k = str(h)
        total = narrow_total("E", k).astype(BF16)
        r["Eg" + k][z] = total
        narrow_hand("E", k)
        gh = total.astype(F32)
        gate = (gh * r["Kg" + k][z, :, :fb].astype(F32)).astype(BF16)
        up = (gh * r["Kg" + k][z, :, fb:2 * fb].astype(F32)).astype(BF16)
        ad = mm_nt(gate, r["bd"][:, :fb]) + mm_nt(up, r["bd"][:, fb:])
        r["adp"][h] = (ADAPTER_SCALE * ad).astype(BF16)

    adapters(0)
    adapters(1)
    for i, device in enumerate(dev_e):
        send("ade", i, r["adp"], r["adre"].at[i], device)
    arrive("fdE")
    fdf = r["fdf"][...].reshape(th, LANES)
    r["dog"][...] = mm_tn(fdf, r["go0"][...])[:RANK] + mm_tn(fdf, r["go1"][...])[RANK:]
    store(r["dog"], dog_o)
    arrive("Grs")
    gff = add_up(r["Gb"][z], r["Gr"], nz - 1).astype(BF16)
    gad = mm_tn(gff, r["hp0"][...])[:RANK] + mm_tn(gff, r["hp1"][...])[RANK:]
    rb, cb = plan.rb, plan.cb
    for j in range(nz):
        r["Mb"][j] = gad[j // 2 * rb:(j // 2 + 1) * rb, j % 2 * cb:(j % 2 + 1) * cb].astype(BF16)
    for i, device in enumerate(dev_z):
        send("Mrs", i, r["Mb"].at[zs[i]], r["Mr"].at[i], device)
    arrive("Kag0")
    arrive("Kag1")
    settle()

    def back(h):
        k = str(h)
        arrive("Eag" + k)
        gh = r["Eg" + k][...].reshape(th, fb).astype(F32)
        kept = r["Kg" + k][...].reshape(th, 2 * fb + LANES)
        r["ggu" + k][:, :fb] = (gh * kept[:, :fb].astype(F32)).astype(BF16)
        r["ggu" + k][:, fb:] = (gh * kept[:, fb:2 * fb].astype(F32)).astype(BF16)
        ggu = r["ggu" + k][...]
        ad = (ADAPTER_SCALE * mm_nt(ggu, r["bd"][...])).astype(BF16)
        gx = mm_nt(ggu, r["wgu"][...]) + mm(ad, r["agu"][...])
        pack(gx.astype(BF16), "F", k)
        scatter_c("F", k)

    back(0)
    arrive("ade")
    r["ads"][...] = add_up(r["adp"][...], r["adre"], ne - 1).astype(BF16)
    for i, device in enumerate(dev_y):
        send("ady", i, r["ads"], r["adry"].at[i], device)
    scatter_x("F", "0")
    back(1)
    scatter_y("F", "0")
    arrive("ady")
    r["adf"][:, z] = add_up(r["ads"][...], r["adry"], ny - 1).astype(BF16)
    for i, device in enumerate(dev_z):
        send("adz", i, r["adf"].at[:, z], r["adf"].at[:, z], device)
    scatter_x("F", "1")
    settle()
    gu = jnp.zeros((LANES, 2 * fb), F32)
    for h in range(2):
        k = str(h)
        factors = r["Kg" + k][:, :, 2 * fb:].reshape(th, LANES)
        gu += mm_tn(factors, r["ggu" + k][...])
    r["gu"][...] = ADAPTER_SCALE * gu
    store(r["gu"].at[:RANK, :fb], gog_o)
    store(r["gu"].at[RANK:, fb:], uog_o)

    def input_gradient(h):
        gx = scatter_end("F", str(h))
        for q in range(NQ):
            r["o32"][2 * h:2 * h + 2, LANES * q:LANES * (q + 1)] = gx[2 * q:2 * q + 2]

    arrive("Mrs")
    r["Mg"][z] = add_up(r["Mb"][z], r["Mr"], nz - 1)
    for i, device in enumerate(dev_z):
        send("Mag", i, r["Mg"].at[z], r["Mg"].at[z], device)
    scatter_y("F", "1")
    arrive("adz")
    r["gab"][...] = mm_tn(r["adf"][...].reshape(2 * th, LANES), r["x"][...])
    store(r["gab"].at[:RANK], ag_o)
    store(r["gab"].at[RANK:], au_o)
    input_gradient(0)
    arrive("Mag")
    for j in range(nz):
        r["gad"][j // 2 * rb:(j // 2 + 1) * rb, j % 2 * cb:(j % 2 + 1) * cb] = r["Mg"][j]
    store(r["gad"], gad_o)
    arrive("dv_")
    dv = add_up(r["dv"][...], r["dvr"], nz - 1)
    for t in range(4):
        dv_o[t] = jnp.max(dv[t:t + 1, :])
    input_gradient(1)
    r["gx"][...] = r["o32"][...].astype(BF16)
    store(r["gx"], gx_o)
    settle()
    for copy in stores:
        copy.wait()


def finish_kernel(*refs):
    srcs, dsts, held, sems = refs[:8], refs[8:16], refs[16:24], refs[24]
    ins = [pltpu.make_async_copy(srcs[i], held[i], sems.at[i]) for i in range(8)]
    outs = [pltpu.make_async_copy(held[i], dsts[i], sems.at[8 + i]) for i in range(8)]
    for copy in ins:
        copy.start()
    for i in range(8):
        ins[i].wait()
        outs[i].start()
    for copy in outs:
        copy.wait()


def shards(wide, narrow, tokens, cotangent, rewards, group_ids, token_mask, w_gate, w_up, down_w,
           a_gate, a_up, gate_of, up_of, a_down, down_of):
    db, fb = w_gate.shape
    plan = Plan(wide, narrow, db, fb)
    hbm = pl.BlockSpec(memory_space=pltpu.HBM)
    sm = pl.BlockSpec(memory_space=pltpu.SMEM)
    s = jax.ShapeDtypeStruct
    shapes = (
        s((4, db), BF16), s((4,), F32), s((RANK, db), F32), s((RANK, db), F32),
        s((RANK, fb), F32), s((RANK, fb), F32), s((RANK, fb), F32), s((RANK, db), F32),
    )
    mids = pl.pallas_call(
        functools.partial(step_kernel, plan),
        out_shape=shapes,
        in_specs=[hbm, hbm, sm, sm, sm] + [hbm] * 9,
        out_specs=(hbm, sm) + (hbm,) * 6,
        scratch_shapes=plan.shapes,
        compiler_params=pltpu.CompilerParams(
            collective_id=0, has_side_effects=True, vmem_limit_bytes=60 << 20),
        name="policy_step",
    )(tokens, cotangent, rewards, group_ids, token_mask, w_gate, w_up, down_w, a_gate.T, a_up.T,
      gate_of, up_of, a_down.T, down_of)
    outs = pl.pallas_call(
        finish_kernel,
        out_shape=shapes,
        in_specs=[hbm] * 8,
        out_specs=(hbm,) * 8,
        scratch_shapes=[pltpu.VMEM(v.shape, v.dtype) for v in shapes]
        + [pltpu.SemaphoreType.DMA((16,))],
        compiler_params=pltpu.CompilerParams(vmem_limit_bytes=60 << 20),
        name="finish",
    )(*mids)
    gx, dv, ag, au, gog, uog, gad, dog = outs
    return gx, dv, ag.T, au.T, gog, uog, gad.T, dog


def solution(mesh):
    return jax.shard_map(
        functools.partial(shards, mesh.shape["wide"], mesh.shape["narrow"]),
        mesh=mesh,
        in_specs=(
            P("wide", "narrow"),
            P("wide", "narrow"),
            P("wide"),
            P("wide"),
            P("wide"),
            P("narrow", "wide"),
            P("narrow", "wide"),
            P("wide", "narrow"),
            P("narrow", None),
            P("narrow", None),
            P(None, "wide"),
            P(None, "wide"),
            P("wide", None),
            P(None, "narrow"),
        ),
        out_specs=(
            P("wide", "narrow"),
            P("wide"),
            P("narrow", None),
            P("narrow", None),
            P(None, "wide"),
            P(None, "wide"),
            P("wide", None),
            P(None, "narrow"),
        ),
        check_vma=False,
    )
```

```python
import functools

import jax
import jax.numpy as jnp
from jax import lax
from jax.experimental import pallas as pl
from jax.experimental.pallas import tpu as pltpu
from jax.sharding import PartitionSpec as P

MESH = pl.DeviceIdType.MESH
BF16 = jnp.bfloat16
F32 = jnp.float32
D = 8192
TOKENS = 256
RANK = 64
ADAPTER_SCALE = 2.0
KL_WEIGHT = 0.1
NQ = 8
LANES = 128


def mm(a, b):
    return jnp.dot(a, b, preferred_element_type=F32)


def mm_nt(a, b):
    return lax.dot_general(a, b, (((1,), (1,)), ((), ())), preferred_element_type=F32)


def mm_tn(a, b):
    return lax.dot_general(a, b, (((0,), (0,)), ((), ())), preferred_element_type=F32)


class Plan:
    def __init__(self, wide, narrow, db, fb):
        self.nx = 4 if wide == 64 else 2
        self.ny = wide // (self.nx * 2)
        self.ne = 2 * self.nx
        self.nz = narrow
        self.wide = wide
        self.db, self.fb = db, fb
        self.th = 2 * wide
        self.tz = self.th // narrow
        self.bs = min(16, wide)
        self.yb = self.bs // self.ne
        self.names, self.shapes = [], []
        nx, ny, nz, ne, th, tz = self.nx, self.ny, self.nz, self.ne, self.th, self.tz
        v = self.vmem
        v("wgu", (db, 2 * fb), BF16)
        v("downx", (fb + LANES, db), BF16)
        v("wgt", (2 * fb, db), BF16)
        v("dnt", (db, fb + LANES), BF16)
        v("agu", (LANES, db), BF16)
        v("bd", (LANES, 2 * fb), BF16)
        v("adown", (RANK, fb), BF16)
        v("tok", (4, db), BF16)
        v("cot", (4, db), BF16)
        v("t32", (2, 16, LANES), F32)
        v("c32", (2, 16, LANES), F32)
        v("o32", (4, db), F32)
        v("x", (2 * th, db), BF16)
        v("gx", (4, db), BF16)
        v("gab", (LANES, db), F32)
        v("gu", (LANES, 2 * fb), F32)
        v("gad", (RANK, fb), F32)
        v("dog", (RANK, db), F32)
        self.dma("load", 12)
        self.dma("out", 7)
        for h in range(2):
            k = str(h)
            for g in "AD":
                v(g + "g" + k, (ny, nx, 2, 16, LANES), BF16)
                self.rem(g + "y" + k, ny - 1)
                self.rem(g + "x" + k, nx - 1)
                self.rem(g + "c" + k, 1)
            for g in "CF":
                v(g + "r" + k, (ny, nx, 2, 16, LANES), BF16)
                v(g + "rc" + k, (ny, nx, 16, LANES), BF16)
                v(g + "s1" + k, (ny, nx, 16, LANES), BF16)
                v(g + "rx" + k, (nx - 1, ny, 16, LANES), BF16)
                v(g + "s2" + k, (ny, 16, LANES), BF16)
                v(g + "ry" + k, (ny - 1, 16, LANES), BF16)
                self.rem(g + "c" + k, 1)
                self.rem(g + "x" + k, nx - 1)
                self.rem(g + "y" + k, ny - 1)
            for g, width in (("B", 2 * fb + LANES), ("E", fb)):
                v(g + "b" + k, (nz, tz, width), BF16)
                v(g + "r" + k, (nz - 1, tz, width), BF16)
                self.rem(g + "rs" + k, nz - 1)
            v("Bl" + k, (tz, fb), BF16)
            v("Bu" + k, (tz, fb + LANES), BF16)
            v("Bq" + k, (2, tz, 2 * fb + LANES), BF16)
            v("Bc" + k, (2, tz, 2 * fb + LANES), BF16)
            for g, count in (("Bl", 1), ("Bu", 1), ("Bq", 2), ("Bd", 2), ("Bc", 2)):
                self.rem(g + k, count)
            for g, width in (("H", fb + LANES), ("K", 2 * fb + LANES), ("E", fb)):
                v(g + "g" + k, (nz, tz, width), BF16)
                self.rem(g + "ag" + k, nz - 1)
            v("hp" + k, (tz, fb), BF16)
            v("go" + k, (th, db), BF16)
            v("ggu" + k, (th, 2 * fb), BF16)
        part = th // ne
        v("fdp", (ne, part, LANES), BF16)
        v("fdre", (ne - 1, part, LANES), BF16)
        v("fds", (part, LANES), BF16)
        v("fdry", (ny - 1, part, LANES), BF16)
        v("fdf", (ne, part, LANES), BF16)
        self.rem("fde", ne - 1)
        self.rem("fdy", ny - 1)
        self.rem("fdE", ne - 1)
        v("adp", (2, tz, LANES), BF16)
        v("adre", (ne - 1, 2, tz, LANES), BF16)
        v("ads", (2, tz, LANES), BF16)
        v("adry", (ny - 1, 2, tz, LANES), BF16)
        v("adf", (2, nz, tz, LANES), BF16)
        self.rem("ade", ne - 1)
        self.rem("ady", ny - 1)
        self.rem("adz", nz - 1)
        v("Gb", (nz, tz, LANES), BF16)
        v("Gr", (nz - 1, tz, LANES), BF16)
        self.rem("Grs", nz - 1)
        self.rb, self.cb = 2 * RANK // nz, fb // 2
        v("Mb", (nz, self.rb, self.cb), BF16)
        v("Mr", (nz - 1, self.rb, self.cb), BF16)
        v("Mg", (nz, self.rb, self.cb), F32)
        self.rem("Mrs", nz - 1)
        self.rem("Mag", nz - 1)
        for name in ("st0", "st1", "dv"):
            v(name, (8, LANES), F32)
        v("ste", (ne - 1, 8, LANES), F32)
        v("sty", (ny - 1, 8, LANES), F32)
        v("dvr", (nz - 1, 8, LANES), F32)
        self.rem("ste_", ne - 1)
        self.rem("sty_", ny - 1)
        self.rem("dv_", nz - 1)

    def vmem(self, name, shape, dtype):
        self.names.append(name)
        self.shapes.append(pltpu.VMEM(shape, dtype))

    def dma(self, name, count):
        self.names.append(name)
        self.shapes.append(pltpu.SemaphoreType.DMA((count,)))

    def rem(self, name, count):
        self.dma(name + ">", count)
        self.dma(name + "<", count)


def step_kernel(plan, *refs):
    (tokens, cotangent, rewards, group_ids, token_mask, w_gate, w_up, down_w, a_gate, a_up,
     gate_of, up_of, a_down, down_of) = refs[:14]
    (gx_o, dv_o, ag_o, au_o, gog_o, uog_o, gad_o, dog_o) = refs[14:22]
    r = dict(zip(plan.names, refs[22:]))
    ny, nx, nz, ne, th, tz, db, fb = (
        plan.ny, plan.nx, plan.nz, plan.ne, plan.th, plan.tz, plan.db, plan.fb)
    w = lax.axis_index("wide")
    z = lax.axis_index("narrow")
    y, x, c = w // ne, (w // 2) % nx, w % 2
    e = w % ne
    other = 1 - c

    def far_first(n):
        return sorted(range(1, n), key=lambda d: -min(d, n - d))

    ys = [(y + d) % ny for d in far_first(ny)]
    xs = [(x + d) % nx for d in far_first(nx)]
    es = [((x + d) % nx) * 2 + v for d in far_first(nx) for v in (c, other)] + [x * 2 + other]
    zs = [(z + d) % nz for d in far_first(nz)]
    dev_y = [(v * ne + e, z) for v in ys]
    dev_x = [(y * ne + v * 2 + c, z) for v in xs]
    dev_e = [(y * ne + v, z) for v in es]
    dev_c = (y * ne + x * 2 + other, z)
    dev_z = [(w, v) for v in zs]
    peers = dev_y + dev_e + dev_z

    barrier = pltpu.get_barrier_semaphore()
    for peer in peers:
        pl.semaphore_signal(barrier, inc=1, device_id=peer, device_id_type=MESH)

    loads = []

    def load(src, dst):
        copy = pltpu.make_async_copy(src, dst, r["load"].at[len(loads)])
        copy.start()
        loads.append(copy)

    load(tokens, r["tok"])
    load(cotangent, r["cot"])

    pending = []
    flying = {}
    stores = []

    def store(src, dst):
        copy = pltpu.make_async_copy(src, dst, r["out"].at[len(stores)])
        copy.start()
        stores.append(copy)

    def send(name, index, src, dst, device):
        copy = pltpu.make_async_remote_copy(
            src_ref=src, dst_ref=dst, send_sem=r[name + ">"].at[index],
            recv_sem=r[name + "<"].at[index], device_id=device, device_id_type=MESH,
        )
        copy.start()
        pending.append(copy)
        flying.setdefault(name, []).append(copy)

    def settle():
        for copy in pending:
            copy.wait_send()
        pending.clear()

    def arrive(name):
        for copy in flying.pop(name):
            copy.wait_recv()

    def add_up(total, slots, count):
        total = total.astype(F32)
        for i in range(count):
            total += slots[i].astype(F32)
        return total

    def gather_y(g, k):
        buf = r[g + "g" + k]
        for i, device in enumerate(dev_y):
            send(g + "y" + k, i, buf.at[y, x, c], buf.at[y, x, c], device)

    def gather_x(g, k):
        buf = r[g + "g" + k]
        arrive(g + "y" + k)
        for i, device in enumerate(dev_x):
            send(g + "x" + k, i, buf.at[:, x, c], buf.at[:, x, c], device)

    def gather_c(g, k):
        buf = r[g + "g" + k]
        arrive(g + "x" + k)
        send(g + "c" + k, 0, buf.at[:, :, c], buf.at[:, :, c], dev_c)

    def scatter_c(g, k):
        buf = r[g + "r" + k]
        send(g + "c" + k, 0, buf.at[:, :, other], r[g + "rc" + k], dev_c)

    def scatter_x(g, k):
        arrive(g + "c" + k)
        total = r[g + "r" + k][:, :, c].astype(F32) + r[g + "rc" + k][...].astype(F32)
        r[g + "s1" + k][...] = total.astype(BF16)
        for i, device in enumerate(dev_x):
            send(g + "x" + k, i, r[g + "s1" + k].at[:, xs[i]], r[g + "rx" + k].at[i], device)

    def scatter_y(g, k):
        arrive(g + "x" + k)
        total = add_up(r[g + "s1" + k][:, x], r[g + "rx" + k], nx - 1)
        r[g + "s2" + k][...] = total.astype(BF16)
        for i, device in enumerate(dev_y):
            send(g + "y" + k, i, r[g + "s2" + k].at[ys[i]], r[g + "ry" + k].at[i], device)

    def scatter_end(g, k):
        arrive(g + "y" + k)
        return add_up(r[g + "s2" + k][y], r[g + "ry" + k], ny - 1)

    def narrow_sum(g, k):
        for i, device in enumerate(dev_z):
            send(g + "rs" + k, i, r[g + "b" + k].at[zs[i]], r[g + "r" + k].at[i], device)

    def narrow_total(g, k):
        arrive(g + "rs" + k)
        return add_up(r[g + "b" + k][z], r[g + "r" + k], nz - 1)

    def at_z(d):
        return (z + d + nz) % nz

    def dev_at(d):
        return (w, at_z(d))

    def ring_sum(k):
        if nz != 8:
            narrow_sum("B", k)
            return
        b = r["Bb" + k]
        send("Bl" + k, 0, b.at[at_z(4), :, :fb], r["Bl" + k], dev_at(2))
        send("Bu" + k, 0, b.at[at_z(4), :, fb:], r["Bu" + k], dev_at(-2))
        for i, sign in enumerate((1, -1)):
            send("Bq" + k, i, b.at[at_z(3 * sign)], r["Bq" + k].at[i], dev_at(sign))
        for i, sign in enumerate((1, -1)):
            send("Bd" + k, i, b.at[at_z(sign)], r["Br" + k].at[i], dev_at(sign))

    def ring_relay(k):
        if nz != 8:
            return
        b = r["Bb" + k]
        for name in ("Bl", "Bu", "Bq"):
            arrive(name + k)
        for i, sign in enumerate((1, -1)):
            both = b[at_z(2 * sign)].astype(F32) + r["Bq" + k][i].astype(F32)
            low, high = both[:, :fb], both[:, fb:]
            if i == 0:
                low += r["Bl" + k][...].astype(F32)
            else:
                high += r["Bu" + k][...].astype(F32)
            r["Bc" + k][i, :, :fb] = low.astype(BF16)
            r["Bc" + k][i, :, fb:] = high.astype(BF16)
            send("Bc" + k, i, r["Bc" + k].at[i], r["Br" + k].at[2 + i], dev_at(2 * sign))

    def ring_total(k):
        if nz != 8:
            return narrow_total("B", k)
        arrive("Bd" + k)
        arrive("Bc" + k)
        return add_up(r["Bb" + k][z], r["Br" + k], 4)

    def narrow_hand(g, k):
        for i, device in enumerate(dev_z):
            send(g + "ag" + k, i, r[g + "g" + k].at[z], r[g + "g" + k].at[z], device)

    def small_row(g):
        for i, device in enumerate(dev_e):
            send(g + "e", i, r[g + "p"].at[es[i]], r[g + "re"].at[i], device)

    def small_y(g):
        arrive(g + "e")
        r[g + "s"][...] = add_up(r[g + "p"][e], r[g + "re"], ne - 1).astype(BF16)
        for i, device in enumerate(dev_y):
            send(g + "y", i, r[g + "s"], r[g + "ry"].at[i], device)

    def small_hand(g):
        arrive(g + "y")
        r[g + "f"][e] = add_up(r[g + "s"][...], r[g + "ry"], ny - 1).astype(BF16)
        for i, device in enumerate(dev_e):
            send(g + "E", i, r[g + "f"].at[e], r[g + "f"].at[e], device)

    loads[0].wait()
    tok = r["tok"][...].astype(F32)
    for h in range(2):
        for q in range(NQ):
            r["t32"][h, 2 * q:2 * q + 2, :] = tok[2 * h:2 * h + 2, LANES * q:LANES * (q + 1)]
        r["Ag" + str(h)][y, x, c] = r["t32"][h].astype(BF16)

    lane = lax.broadcasted_iota(jnp.int32, (1, LANES), 1)
    mask = [token_mask[t].astype(F32) for t in range(4)]
    reward = [rewards[t] for t in range(4)]
    ids = [group_ids[t] for t in range(4)]
    reward_row = jnp.zeros((1, LANES), F32)
    count_row = jnp.zeros((1, LANES), F32)
    for t in range(4):
        reward_row += jnp.where(lane == ids[t], mask[t] * reward[t], 0.0)
        count_row += jnp.where(lane == ids[t], mask[t], 0.0)
    row8 = lax.broadcasted_iota(jnp.int32, (8, LANES), 0)
    r["st0"][...] = jnp.where(row8 == 0, reward_row, jnp.where(row8 == 1, count_row, 0.0))

    pl.semaphore_wait(barrier, len(peers))
    gather_y("A", "0")
    gather_y("A", "1")
    for i, device in enumerate(dev_e):
        send("ste_", i, r["st0"], r["ste"].at[i], device)
    load(w_gate, r["wgu"].at[:, :fb])
    load(w_up, r["wgu"].at[:, fb:])
    load(a_gate, r["agu"].at[:RANK])
    load(a_up, r["agu"].at[RANK:])
    load(gate_of, r["bd"].at[:RANK, :fb])
    load(up_of, r["bd"].at[RANK:, fb:])
    load(down_w, r["downx"].at[:fb])
    load(down_of, r["downx"].at[fb:fb + RANK])
    load(down_of, r["downx"].at[fb + RANK:])
    load(a_down, r["adown"])

    rows = plan.bs * 16
    row = lax.broadcasted_iota(jnp.int32, (rows, rows), 0)
    col = lax.broadcasted_iota(jnp.int32, (rows, rows), 1)

    def by_block(v):
        return ((v >> 1) & 7) * (2 * plan.bs) + (v >> 4) * 2 + (v & 1)

    to_tokens = (row == by_block(col)).astype(F32).astype(BF16)
    to_shards = (col == by_block(row)).astype(F32).astype(BF16)

    def unpack(g, k, out, base):
        for b in range(plan.wide // plan.bs):
            block = r[g + "g" + k][plan.yb * b:plan.yb * (b + 1)].reshape(rows, LANES)
            turned = mm(to_tokens, block).astype(BF16)
            n = 2 * plan.bs
            for q in range(NQ):
                out[base + n * b:base + n * (b + 1), LANES * q:LANES * (q + 1)] = (
                    turned[n * q:n * (q + 1)])

    def pack(value, g, k):
        for b in range(plan.wide // plan.bs):
            n = 2 * plan.bs
            block = jnp.concatenate(
                [value[n * b:n * (b + 1), LANES * q:LANES * (q + 1)] for q in range(NQ)], axis=0)
            turned = mm(to_shards, block).astype(BF16)
            r[g + "r" + k][plan.yb * b:plan.yb * (b + 1)] = turned.reshape(
                plan.yb, nx, 2, 16, LANES)

    loads[1].wait()
    cot = r["cot"][...].astype(F32)
    for h in range(2):
        for q in range(NQ):
            r["c32"][h, 2 * q:2 * q + 2, :] = cot[2 * h:2 * h + 2, LANES * q:LANES * (q + 1)]
    r["bd"][:RANK, fb:] = jnp.zeros((RANK, fb), BF16)
    r["bd"][RANK:, :fb] = jnp.zeros((RANK, fb), BF16)
    gather_x("A", "0")
    gather_x("A", "1")

    arrive("ste_")
    r["st1"][...] = add_up(r["st0"][...], r["ste"], ne - 1)
    for i, device in enumerate(dev_y):
        send("sty_", i, r["st1"], r["sty"].at[i], device)
    for i in range(2, 8):
        loads[i].wait()
    gather_c("A", "0")
    gather_c("A", "1")

    def project(h):
        k = str(h)
        arrive("Ac" + k)
        unpack("A", k, r["x"], h * th)
        xv = r["x"][h * th:(h + 1) * th]
        r["Bb" + k][:, :, 2 * fb:] = (
            mm_nt(xv, r["agu"][...]).astype(BF16).reshape(nz, tz, LANES))
        r["Bb" + k][:, :, :2 * fb] = (
            mm(xv, r["wgu"][...]).astype(BF16).reshape(nz, tz, 2 * fb))
        ring_sum(k)

    def turn(src, dst, begin, end):
        for i in range(begin, end, db // 8):
            dst[:, i:i + db // 8] = src[i:i + db // 8, :].T

    project(0)
    project(1)
    turn(r["wgu"], r["wgt"], 0, db // 2)
    ring_relay("0")

    arrive("sty_")
    stats = add_up(r["st1"][...], r["sty"], ny - 1)
    group_count = stats[1:2]
    group_mean = stats[0:1] / jnp.maximum(group_count, 1.0)
    all_count = jnp.sum(group_count, axis=1, keepdims=True)
    scale_of = TOKENS / jnp.maximum(all_count, 1.0)
    advantage, token_scale = [], []
    for t in range(4):
        mean_t = jnp.sum(jnp.where(lane == ids[t], group_mean, 0.0), axis=1, keepdims=True)
        advantage.append(reward[t] - mean_t)
        token_scale.append(mask[t] * scale_of)
    loads[11].wait()
    ring_relay("1")
    turn(r["wgu"], r["wgt"], db // 2, db)

    def hidden(h):
        k = str(h)
        total = ring_total(k)
        factors = total[:, 2 * fb:].astype(BF16)
        adapt = ADAPTER_SCALE * mm(factors, r["bd"][...])
        gate_base = total[:, :fb]
        up_base = total[:, fb:2 * fb]
        gate = gate_base + adapt[:, :fb]
        up = up_base + adapt[:, fb:]
        sig = jax.nn.sigmoid(gate)
        silu = gate * sig
        slope = sig * (1.0 + gate * (1.0 - sig))
        full = silu * up
        hp = full.astype(BF16)
        hd = (full - gate_base * jax.nn.sigmoid(gate_base) * up_base).astype(BF16)
        fd = ADAPTER_SCALE * mm_nt(hp, r["adown"][...])
        none = jnp.zeros_like(fd)
        fd = jnp.concatenate([none, fd] if h else [fd, none], axis=1)
        r["Hg" + k][z, :, :fb] = hd
        r["Hg" + k][z, :, fb:] = fd.astype(BF16)
        narrow_hand("H", k)
        r["Kg" + k][z, :, :fb] = (up * slope).astype(BF16)
        r["Kg" + k][z, :, fb:2 * fb] = silu.astype(BF16)
        r["Kg" + k][z, :, 2 * fb:] = factors
        r["hp" + k][...] = hp

    hidden(0)
    hidden(1)
    for i in range(8, 11):
        loads[i].wait()
    turn(r["downx"], r["dnt"], 0, fb + LANES)

    def outward(h):
        k = str(h)
        arrive("Hag" + k)
        both = r["Hg" + k][...].reshape(th, fb + LANES)
        pack(mm(both, r["downx"][...]).astype(BF16), "C", k)
        scatter_c("C", k)
        return both[:, fb:].astype(F32)

    row16 = lax.broadcasted_iota(jnp.int32, (16, 1), 0)
    even = (row16 & 1) == 0
    div = []

    def gradient(h):
        k = str(h)
        od = scatter_end("C", k)
        adv = jnp.where(even, advantage[2 * h], advantage[2 * h + 1])
        scl = jnp.where(even, token_scale[2 * h], token_scale[2 * h + 1])
        grad = scl * (KL_WEIGHT * od - adv * r["c32"][h])
        r["Dg" + k][y, x, c] = grad.astype(BF16)
        gather_y("D", k)
        square = od * od
        for t in range(2):
            picked = jnp.where(((row16 & 1) == t), square, 0.0)
            div.append(jnp.sum(jnp.sum(picked, axis=1, keepdims=True), axis=0, keepdims=True))

    fd0 = outward(0)
    scatter_x("C", "0")
    fd1 = outward(1)
    settle()
    narrow_hand("K", "0")
    r["fdp"][...] = (fd0 + fd1).astype(BF16).reshape(ne, th // ne, LANES)
    small_row("fd")
    scatter_y("C", "0")
    scatter_x("C", "1")
    gradient(0)
    narrow_hand("K", "1")
    scatter_y("C", "1")
    small_y("fd")
    gather_x("D", "0")
    gradient(1)
    dv = jnp.zeros((8, LANES), F32)
    for t in range(4):
        dv += jnp.where(row8 == t, div[t], 0.0)
    r["dv"][...] = dv * (0.5 / D)
    for i, device in enumerate(dev_z):
        send("dv_", i, r["dv"], r["dvr"].at[i], device)
    gather_c("D", "0")
    gather_x("D", "1")
    small_hand("fd")
    settle()

    def inward(h):
        k = str(h)
        arrive("Dc" + k)
        unpack("D", k, r["go" + k], 0)
        both = mm(r["go" + k][...], r["dnt"][...])
        gf = ADAPTER_SCALE * both[:, fb:]
        gh = both[:, :fb] + mm(gf[:, :RANK].astype(BF16), r["adown"][...])
        r["Eb" + k][...] = gh.astype(BF16).reshape(nz, tz, fb)
        narrow_sum("E", k)
        return gf

    gf0 = inward(0)
    gather_c("D", "1")
    gf1 = inward(1)
    r["Gb"][...] = jnp.where(lane < RANK, gf0, gf1).astype(BF16).reshape(nz, tz, LANES)
    for i, device in enumerate(dev_z):
        send("Grs", i, r["Gb"].at[zs[i]], r["Gr"].at[i], device)
    def adapters(h):
        k = str(h)
        total = narrow_total("E", k).astype(BF16)
        r["Eg" + k][z] = total
        narrow_hand("E", k)
        gh = total.astype(F32)
        gate = (gh * r["Kg" + k][z, :, :fb].astype(F32)).astype(BF16)
        up = (gh * r["Kg" + k][z, :, fb:2 * fb].astype(F32)).astype(BF16)
        ad = mm_nt(gate, r["bd"][:, :fb]) + mm_nt(up, r["bd"][:, fb:])
        r["adp"][h] = (ADAPTER_SCALE * ad).astype(BF16)

    adapters(0)
    adapters(1)
    for i, device in enumerate(dev_e):
        send("ade", i, r["adp"], r["adre"].at[i], device)
    arrive("fdE")
    fdf = r["fdf"][...].reshape(th, LANES)
    r["dog"][...] = mm_tn(fdf, r["go0"][...])[:RANK] + mm_tn(fdf, r["go1"][...])[RANK:]
    store(r["dog"], dog_o)
    arrive("Grs")
    gff = add_up(r["Gb"][z], r["Gr"], nz - 1).astype(BF16)
    gad = mm_tn(gff, r["hp0"][...])[:RANK] + mm_tn(gff, r["hp1"][...])[RANK:]
    rb, cb = plan.rb, plan.cb
    for j in range(nz):
        r["Mb"][j] = gad[j // 2 * rb:(j // 2 + 1) * rb, j % 2 * cb:(j % 2 + 1) * cb].astype(BF16)
    for i, device in enumerate(dev_z):
        send("Mrs", i, r["Mb"].at[zs[i]], r["Mr"].at[i], device)
    arrive("Kag0")
    arrive("Kag1")
    settle()

    def back(h):
        k = str(h)
        arrive("Eag" + k)
        gh = r["Eg" + k][...].reshape(th, fb).astype(F32)
        kept = r["Kg" + k][...].reshape(th, 2 * fb + LANES)
        r["ggu" + k][:, :fb] = (gh * kept[:, :fb].astype(F32)).astype(BF16)
        r["ggu" + k][:, fb:] = (gh * kept[:, fb:2 * fb].astype(F32)).astype(BF16)
        ggu = r["ggu" + k][...]
        ad = (ADAPTER_SCALE * mm_nt(ggu, r["bd"][...])).astype(BF16)
        gx = mm(ggu, r["wgt"][...]) + mm(ad, r["agu"][...])
        pack(gx.astype(BF16), "F", k)
        scatter_c("F", k)

    back(0)
    arrive("ade")
    r["ads"][...] = add_up(r["adp"][...], r["adre"], ne - 1).astype(BF16)
    for i, device in enumerate(dev_y):
        send("ady", i, r["ads"], r["adry"].at[i], device)
    scatter_x("F", "0")
    back(1)
    scatter_y("F", "0")
    arrive("ady")
    r["adf"][:, z] = add_up(r["ads"][...], r["adry"], ny - 1).astype(BF16)
    for i, device in enumerate(dev_z):
        send("adz", i, r["adf"].at[:, z], r["adf"].at[:, z], device)
    scatter_x("F", "1")
    settle()
    gu = jnp.zeros((LANES, 2 * fb), F32)
    for h in range(2):
        k = str(h)
        factors = r["Kg" + k][:, :, 2 * fb:].reshape(th, LANES)
        gu += mm_tn(factors, r["ggu" + k][...])
    r["gu"][...] = ADAPTER_SCALE * gu
    store(r["gu"].at[:RANK, :fb], gog_o)
    store(r["gu"].at[RANK:, fb:], uog_o)

    def input_gradient(h):
        gx = scatter_end("F", str(h))
        for q in range(NQ):
            r["o32"][2 * h:2 * h + 2, LANES * q:LANES * (q + 1)] = gx[2 * q:2 * q + 2]

    arrive("Mrs")
    r["Mg"][z] = add_up(r["Mb"][z], r["Mr"], nz - 1)
    for i, device in enumerate(dev_z):
        send("Mag", i, r["Mg"].at[z], r["Mg"].at[z], device)
    scatter_y("F", "1")
    arrive("adz")
    r["gab"][...] = mm_tn(r["adf"][...].reshape(2 * th, LANES), r["x"][...])
    store(r["gab"].at[:RANK], ag_o)
    store(r["gab"].at[RANK:], au_o)
    input_gradient(0)
    arrive("Mag")
    for j in range(nz):
        r["gad"][j // 2 * rb:(j // 2 + 1) * rb, j % 2 * cb:(j % 2 + 1) * cb] = r["Mg"][j]
    store(r["gad"], gad_o)
    arrive("dv_")
    dv = add_up(r["dv"][...], r["dvr"], nz - 1)
    for t in range(4):
        dv_o[t] = jnp.max(dv[t:t + 1, :])
    input_gradient(1)
    r["gx"][...] = r["o32"][...].astype(BF16)
    store(r["gx"], gx_o)
    settle()
    for copy in stores:
        copy.wait()


def finish_kernel(*refs):
    srcs, dsts, held, sems = refs[:8], refs[8:16], refs[16:24], refs[24]
    ins = [pltpu.make_async_copy(srcs[i], held[i], sems.at[i]) for i in range(8)]
    outs = [pltpu.make_async_copy(held[i], dsts[i], sems.at[8 + i]) for i in range(8)]
    for copy in ins:
        copy.start()
    for i in range(8):
        ins[i].wait()
        outs[i].start()
    for copy in outs:
        copy.wait()


def shards(wide, narrow, tokens, cotangent, rewards, group_ids, token_mask, w_gate, w_up, down_w,
           a_gate, a_up, gate_of, up_of, a_down, down_of):
    db, fb = w_gate.shape
    plan = Plan(wide, narrow, db, fb)
    hbm = pl.BlockSpec(memory_space=pltpu.HBM)
    sm = pl.BlockSpec(memory_space=pltpu.SMEM)
    s = jax.ShapeDtypeStruct
    shapes = (
        s((4, db), BF16), s((4,), F32), s((RANK, db), F32), s((RANK, db), F32),
        s((RANK, fb), F32), s((RANK, fb), F32), s((RANK, fb), F32), s((RANK, db), F32),
    )
    mids = pl.pallas_call(
        functools.partial(step_kernel, plan),
        out_shape=shapes,
        in_specs=[hbm, hbm, sm, sm, sm] + [hbm] * 9,
        out_specs=(hbm, sm) + (hbm,) * 6,
        scratch_shapes=plan.shapes,
        compiler_params=pltpu.CompilerParams(
            collective_id=0, has_side_effects=True, vmem_limit_bytes=60 << 20),
        name="policy_step",
    )(tokens, cotangent, rewards, group_ids, token_mask, w_gate, w_up, down_w, a_gate.T, a_up.T,
      gate_of, up_of, a_down.T, down_of)
    outs = pl.pallas_call(
        finish_kernel,
        out_shape=shapes,
        in_specs=[hbm] * 8,
        out_specs=(hbm,) * 8,
        scratch_shapes=[pltpu.VMEM(v.shape, v.dtype) for v in shapes]
        + [pltpu.SemaphoreType.DMA((16,))],
        compiler_params=pltpu.CompilerParams(vmem_limit_bytes=60 << 20),
        name="finish",
    )(*mids)
    gx, dv, ag, au, gog, uog, gad, dog = outs
    return gx, dv, ag.T, au.T, gog, uog, gad.T, dog


def solution(mesh):
    return jax.shard_map(
        functools.partial(shards, mesh.shape["wide"], mesh.shape["narrow"]),
        mesh=mesh,
        in_specs=(
            P("wide", "narrow"),
            P("wide", "narrow"),
            P("wide"),
            P("wide"),
            P("wide"),
            P("narrow", "wide"),
            P("narrow", "wide"),
            P("wide", "narrow"),
            P("narrow", None),
            P("narrow", None),
            P(None, "wide"),
            P(None, "wide"),
            P("wide", None),
            P(None, "narrow"),
        ),
        out_specs=(
            P("wide", "narrow"),
            P("wide"),
            P("narrow", None),
            P("narrow", None),
            P(None, "wide"),
            P(None, "wide"),
            P("wide", None),
            P(None, "narrow"),
        ),
        check_vma=False,
    )
```

```python
import functools

import jax
import jax.numpy as jnp
from jax import lax
from jax.experimental import pallas as pl
from jax.experimental.pallas import tpu as pltpu
from jax.sharding import PartitionSpec as P

MESH = pl.DeviceIdType.MESH
BF16 = jnp.bfloat16
F32 = jnp.float32
D = 8192
TOKENS = 256
RANK = 64
ADAPTER_SCALE = 2.0
KL_WEIGHT = 0.1
NQ = 8
LANES = 128


def mm(a, b):
    return jnp.dot(a, b, preferred_element_type=F32)


def mm_nt(a, b):
    return lax.dot_general(a, b, (((1,), (1,)), ((), ())), preferred_element_type=F32)


def mm_tn(a, b):
    return lax.dot_general(a, b, (((0,), (0,)), ((), ())), preferred_element_type=F32)


class Plan:
    def __init__(self, wide, narrow, db, fb):
        self.nx = 4 if wide == 64 else 2
        self.ny = wide // (self.nx * 2)
        self.ne = 2 * self.nx
        self.nz = narrow
        self.wide = wide
        self.db, self.fb = db, fb
        self.th = 2 * wide
        self.tz = self.th // narrow
        self.bs = min(16, wide)
        self.yb = self.bs // self.ne
        self.names, self.shapes = [], []
        nx, ny, nz, ne, th, tz = self.nx, self.ny, self.nz, self.ne, self.th, self.tz
        v = self.vmem
        v("wgu", (db, 2 * fb), BF16)
        v("downx", (fb + LANES, db), BF16)
        v("wgt", (2 * fb, db), BF16)
        v("dnt", (db, fb + LANES), BF16)
        v("agu", (LANES, db), BF16)
        v("bd", (LANES, 2 * fb), BF16)
        v("adown", (RANK, fb), BF16)
        v("tok", (4, db), BF16)
        v("cot", (4, db), BF16)
        v("t32", (2, 16, LANES), F32)
        v("c32", (2, 16, LANES), F32)
        v("o32", (4, db), F32)
        v("x", (2 * th, db), BF16)
        v("gx", (4, db), BF16)
        v("gab", (LANES, db), F32)
        v("gu", (LANES, 2 * fb), F32)
        v("gad", (RANK, fb), F32)
        v("dog", (RANK, db), F32)
        self.dma("load", 12)
        self.dma("out", 7)
        for h in range(2):
            k = str(h)
            for g in "AD":
                v(g + "g" + k, (ny, nx, 2, 16, LANES), BF16)
                self.rem(g + "y" + k, ny - 1)
                self.rem(g + "x" + k, nx - 1)
                self.rem(g + "c" + k, 1)
            for g in "CF":
                v(g + "r" + k, (ny, nx, 2, 16, LANES), BF16)
                v(g + "rc" + k, (ny, nx, 16, LANES), BF16)
                v(g + "s1" + k, (ny, nx, 16, LANES), BF16)
                v(g + "rx" + k, (nx - 1, ny, 16, LANES), BF16)
                v(g + "s2" + k, (ny, 16, LANES), BF16)
                v(g + "ry" + k, (ny - 1, 16, LANES), BF16)
                self.rem(g + "c" + k, 1)
                self.rem(g + "x" + k, nx - 1)
                self.rem(g + "y" + k, ny - 1)
            for g, width in (("B", 2 * fb + LANES), ("E", fb)):
                v(g + "b" + k, (nz, tz, width), BF16)
                v(g + "r" + k, (nz - 1, tz, width), BF16)
                self.rem(g + "rs" + k, nz - 1)
            v("Bl" + k, (tz, fb), BF16)
            v("Bu" + k, (tz, fb + LANES), BF16)
            v("Bq" + k, (2, tz, 2 * fb + LANES), BF16)
            v("Bc" + k, (2, tz, 2 * fb + LANES), BF16)
            for g, count in (("Bl", 1), ("Bu", 1), ("Bq", 2), ("Bd", 2), ("Bc", 2)):
                self.rem(g + k, count)
            for g, width in (("H", fb + LANES), ("K", 2 * fb + LANES), ("E", fb)):
                v(g + "g" + k, (nz, tz, width), BF16)
                self.rem(g + "ag" + k, nz - 1)
            v("hp" + k, (tz, fb), BF16)
            v("go" + k, (th, db), BF16)
            v("ggu" + k, (th, 2 * fb), BF16)
        part = th // ne
        v("fdp", (ne, part, LANES), BF16)
        v("fdre", (ne - 1, part, LANES), BF16)
        v("fds", (part, LANES), BF16)
        v("fdry", (ny - 1, part, LANES), BF16)
        v("fdf", (ne, part, LANES), BF16)
        self.rem("fde", ne - 1)
        self.rem("fdy", ny - 1)
        self.rem("fdE", ne - 1)
        v("adp", (2, tz, LANES), BF16)
        v("adre", (ne - 1, 2, tz, LANES), BF16)
        v("ads", (2, tz, LANES), BF16)
        v("adry", (ny - 1, 2, tz, LANES), BF16)
        v("adf", (2, nz, tz, LANES), BF16)
        self.rem("ade", ne - 1)
        self.rem("ady", ny - 1)
        self.rem("adz", nz - 1)
        v("Gb", (nz, tz, LANES), BF16)
        v("Gr", (nz - 1, tz, LANES), BF16)
        self.rem("Grs", nz - 1)
        self.rb, self.cb = 2 * RANK // nz, fb // 2
        v("Mb", (nz, self.rb, self.cb), BF16)
        v("Mr", (nz - 1, self.rb, self.cb), BF16)
        v("Mg", (nz, self.rb, self.cb), F32)
        self.rem("Mrs", nz - 1)
        self.rem("Mag", nz - 1)
        for name in ("st0", "st1", "dv"):
            v(name, (8, LANES), F32)
        v("ste", (ne - 1, 8, LANES), F32)
        v("sty", (ny - 1, 8, LANES), F32)
        v("dvr", (nz - 1, 8, LANES), F32)
        self.rem("ste_", ne - 1)
        self.rem("sty_", ny - 1)
        self.rem("dv_", nz - 1)

    def vmem(self, name, shape, dtype):
        self.names.append(name)
        self.shapes.append(pltpu.VMEM(shape, dtype))

    def dma(self, name, count):
        self.names.append(name)
        self.shapes.append(pltpu.SemaphoreType.DMA((count,)))

    def rem(self, name, count):
        self.dma(name + ">", count)
        self.dma(name + "<", count)


def step_kernel(plan, *refs):
    (tokens, cotangent, rewards, group_ids, token_mask, w_gate, w_up, down_w, a_gate, a_up,
     gate_of, up_of, a_down, down_of) = refs[:14]
    (gx_o, dv_o, ag_o, au_o, gog_o, uog_o, gad_o, dog_o) = refs[14:22]
    r = dict(zip(plan.names, refs[22:]))
    ny, nx, nz, ne, th, tz, db, fb = (
        plan.ny, plan.nx, plan.nz, plan.ne, plan.th, plan.tz, plan.db, plan.fb)
    w = lax.axis_index("wide")
    z = lax.axis_index("narrow")
    y, x, c = w // ne, (w // 2) % nx, w % 2
    e = w % ne
    other = 1 - c

    def far_first(n):
        return sorted(range(1, n), key=lambda d: -min(d, n - d))

    ys = [(y + d) % ny for d in far_first(ny)]
    xs = [(x + d) % nx for d in far_first(nx)]
    es = [((x + d) % nx) * 2 + v for d in far_first(nx) for v in (c, other)] + [x * 2 + other]
    zs = [(z + d) % nz for d in far_first(nz)]
    dev_y = [(v * ne + e, z) for v in ys]
    dev_x = [(y * ne + v * 2 + c, z) for v in xs]
    dev_e = [(y * ne + v, z) for v in es]
    dev_c = (y * ne + x * 2 + other, z)
    dev_z = [(w, v) for v in zs]
    peers = dev_y + dev_e + dev_z

    barrier = pltpu.get_barrier_semaphore()
    for peer in peers:
        pl.semaphore_signal(barrier, inc=1, device_id=peer, device_id_type=MESH)

    loads = []

    def load(src, dst):
        copy = pltpu.make_async_copy(src, dst, r["load"].at[len(loads)])
        copy.start()
        loads.append(copy)

    load(tokens, r["tok"])
    load(cotangent, r["cot"])

    pending = []
    flying = {}
    stores = []

    def store(src, dst):
        copy = pltpu.make_async_copy(src, dst, r["out"].at[len(stores)])
        copy.start()
        stores.append(copy)

    def send(name, index, src, dst, device):
        copy = pltpu.make_async_remote_copy(
            src_ref=src, dst_ref=dst, send_sem=r[name + ">"].at[index],
            recv_sem=r[name + "<"].at[index], device_id=device, device_id_type=MESH,
        )
        copy.start()
        pending.append(copy)
        flying.setdefault(name, []).append(copy)

    def settle(keep=0):
        for copy in pending[:len(pending) - keep]:
            copy.wait_send()
        del pending[:len(pending) - keep]

    def arrive(name):
        for copy in flying.pop(name):
            copy.wait_recv()

    def add_up(total, slots, count):
        total = total.astype(F32)
        for i in range(count):
            total += slots[i].astype(F32)
        return total

    def gather_y(g, k):
        buf = r[g + "g" + k]
        for i, device in enumerate(dev_y):
            send(g + "y" + k, i, buf.at[y, x, c], buf.at[y, x, c], device)

    def gather_x(g, k):
        buf = r[g + "g" + k]
        arrive(g + "y" + k)
        for i, device in enumerate(dev_x):
            send(g + "x" + k, i, buf.at[:, x, c], buf.at[:, x, c], device)

    def gather_c(g, k):
        buf = r[g + "g" + k]
        arrive(g + "x" + k)
        send(g + "c" + k, 0, buf.at[:, :, c], buf.at[:, :, c], dev_c)

    def scatter_c(g, k):
        buf = r[g + "r" + k]
        send(g + "c" + k, 0, buf.at[:, :, other], r[g + "rc" + k], dev_c)

    def scatter_x(g, k):
        arrive(g + "c" + k)
        total = r[g + "r" + k][:, :, c].astype(F32) + r[g + "rc" + k][...].astype(F32)
        r[g + "s1" + k][...] = total.astype(BF16)
        for i, device in enumerate(dev_x):
            send(g + "x" + k, i, r[g + "s1" + k].at[:, xs[i]], r[g + "rx" + k].at[i], device)

    def scatter_y(g, k):
        arrive(g + "x" + k)
        total = add_up(r[g + "s1" + k][:, x], r[g + "rx" + k], nx - 1)
        r[g + "s2" + k][...] = total.astype(BF16)
        for i, device in enumerate(dev_y):
            send(g + "y" + k, i, r[g + "s2" + k].at[ys[i]], r[g + "ry" + k].at[i], device)

    def scatter_end(g, k):
        arrive(g + "y" + k)
        return add_up(r[g + "s2" + k][y], r[g + "ry" + k], ny - 1)

    def narrow_sum(g, k):
        for i, device in enumerate(dev_z):
            send(g + "rs" + k, i, r[g + "b" + k].at[zs[i]], r[g + "r" + k].at[i], device)

    def narrow_total(g, k):
        arrive(g + "rs" + k)
        return add_up(r[g + "b" + k][z], r[g + "r" + k], nz - 1)

    def at_z(d):
        return (z + d + nz) % nz

    def dev_at(d):
        return (w, at_z(d))

    def ring_sum(k):
        if nz != 8:
            narrow_sum("B", k)
            return
        b = r["Bb" + k]
        send("Bl" + k, 0, b.at[at_z(4), :, :fb], r["Bl" + k], dev_at(2))
        send("Bu" + k, 0, b.at[at_z(4), :, fb:], r["Bu" + k], dev_at(-2))
        for i, sign in enumerate((1, -1)):
            send("Bq" + k, i, b.at[at_z(3 * sign)], r["Bq" + k].at[i], dev_at(sign))
        for i, sign in enumerate((1, -1)):
            send("Bd" + k, i, b.at[at_z(sign)], r["Br" + k].at[i], dev_at(sign))

    def ring_relay(k):
        if nz != 8:
            return
        b = r["Bb" + k]
        for name in ("Bl", "Bu", "Bq"):
            arrive(name + k)
        for i, sign in enumerate((1, -1)):
            both = b[at_z(2 * sign)].astype(F32) + r["Bq" + k][i].astype(F32)
            low, high = both[:, :fb], both[:, fb:]
            if i == 0:
                low += r["Bl" + k][...].astype(F32)
            else:
                high += r["Bu" + k][...].astype(F32)
            r["Bc" + k][i, :, :fb] = low.astype(BF16)
            r["Bc" + k][i, :, fb:] = high.astype(BF16)
            send("Bc" + k, i, r["Bc" + k].at[i], r["Br" + k].at[2 + i], dev_at(2 * sign))

    def ring_total(k):
        if nz != 8:
            return narrow_total("B", k)
        arrive("Bd" + k)
        arrive("Bc" + k)
        return add_up(r["Bb" + k][z], r["Br" + k], 4)

    def narrow_hand(g, k):
        for i, device in enumerate(dev_z):
            send(g + "ag" + k, i, r[g + "g" + k].at[z], r[g + "g" + k].at[z], device)

    def small_row(g):
        for i, device in enumerate(dev_e):
            send(g + "e", i, r[g + "p"].at[es[i]], r[g + "re"].at[i], device)

    def small_y(g):
        arrive(g + "e")
        r[g + "s"][...] = add_up(r[g + "p"][e], r[g + "re"], ne - 1).astype(BF16)
        for i, device in enumerate(dev_y):
            send(g + "y", i, r[g + "s"], r[g + "ry"].at[i], device)

    def small_hand(g):
        arrive(g + "y")
        r[g + "f"][e] = add_up(r[g + "s"][...], r[g + "ry"], ny - 1).astype(BF16)
        for i, device in enumerate(dev_e):
            send(g + "E", i, r[g + "f"].at[e], r[g + "f"].at[e], device)

    loads[0].wait()
    tok = r["tok"][...].astype(F32)
    for h in range(2):
        for q in range(NQ):
            r["t32"][h, 2 * q:2 * q + 2, :] = tok[2 * h:2 * h + 2, LANES * q:LANES * (q + 1)]
        r["Ag" + str(h)][y, x, c] = r["t32"][h].astype(BF16)

    lane = lax.broadcasted_iota(jnp.int32, (1, LANES), 1)
    mask = [token_mask[t].astype(F32) for t in range(4)]
    reward = [rewards[t] for t in range(4)]
    ids = [group_ids[t] for t in range(4)]
    reward_row = jnp.zeros((1, LANES), F32)
    count_row = jnp.zeros((1, LANES), F32)
    for t in range(4):
        reward_row += jnp.where(lane == ids[t], mask[t] * reward[t], 0.0)
        count_row += jnp.where(lane == ids[t], mask[t], 0.0)
    row8 = lax.broadcasted_iota(jnp.int32, (8, LANES), 0)
    r["st0"][...] = jnp.where(row8 == 0, reward_row, jnp.where(row8 == 1, count_row, 0.0))

    pl.semaphore_wait(barrier, len(peers))
    gather_y("A", "0")
    gather_y("A", "1")
    for i, device in enumerate(dev_e):
        send("ste_", i, r["st0"], r["ste"].at[i], device)
    load(w_gate, r["wgu"].at[:, :fb])
    load(w_up, r["wgu"].at[:, fb:])
    load(a_gate, r["agu"].at[:RANK])
    load(a_up, r["agu"].at[RANK:])
    load(gate_of, r["bd"].at[:RANK, :fb])
    load(up_of, r["bd"].at[RANK:, fb:])
    load(down_w, r["downx"].at[:fb])
    load(down_of, r["downx"].at[fb:fb + RANK])
    load(down_of, r["downx"].at[fb + RANK:])
    load(a_down, r["adown"])

    rows = plan.bs * 16
    row = lax.broadcasted_iota(jnp.int32, (rows, rows), 0)
    col = lax.broadcasted_iota(jnp.int32, (rows, rows), 1)

    def by_block(v):
        return ((v >> 1) & 7) * (2 * plan.bs) + (v >> 4) * 2 + (v & 1)

    to_tokens = (row == by_block(col)).astype(F32).astype(BF16)
    to_shards = (col == by_block(row)).astype(F32).astype(BF16)

    def unpack(g, k, out, base):
        for b in range(plan.wide // plan.bs):
            block = r[g + "g" + k][plan.yb * b:plan.yb * (b + 1)].reshape(rows, LANES)
            turned = mm(to_tokens, block).astype(BF16)
            n = 2 * plan.bs
            for q in range(NQ):
                out[base + n * b:base + n * (b + 1), LANES * q:LANES * (q + 1)] = (
                    turned[n * q:n * (q + 1)])

    def pack(value, g, k):
        for b in range(plan.wide // plan.bs):
            n = 2 * plan.bs
            block = jnp.concatenate(
                [value[n * b:n * (b + 1), LANES * q:LANES * (q + 1)] for q in range(NQ)], axis=0)
            turned = mm(to_shards, block).astype(BF16)
            r[g + "r" + k][plan.yb * b:plan.yb * (b + 1)] = turned.reshape(
                plan.yb, nx, 2, 16, LANES)

    loads[1].wait()
    cot = r["cot"][...].astype(F32)
    for h in range(2):
        for q in range(NQ):
            r["c32"][h, 2 * q:2 * q + 2, :] = cot[2 * h:2 * h + 2, LANES * q:LANES * (q + 1)]
    r["bd"][:RANK, fb:] = jnp.zeros((RANK, fb), BF16)
    r["bd"][RANK:, :fb] = jnp.zeros((RANK, fb), BF16)
    gather_x("A", "0")
    gather_x("A", "1")

    arrive("ste_")
    r["st1"][...] = add_up(r["st0"][...], r["ste"], ne - 1)
    for i, device in enumerate(dev_y):
        send("sty_", i, r["st1"], r["sty"].at[i], device)
    for i in range(2, 8):
        loads[i].wait()
    gather_c("A", "0")
    gather_c("A", "1")

    def project(h):
        k = str(h)
        arrive("Ac" + k)
        unpack("A", k, r["x"], h * th)
        xv = r["x"][h * th:(h + 1) * th]
        r["Bb" + k][:, :, 2 * fb:] = (
            mm_nt(xv, r["agu"][...]).astype(BF16).reshape(nz, tz, LANES))
        r["Bb" + k][:, :, :2 * fb] = (
            mm(xv, r["wgu"][...]).astype(BF16).reshape(nz, tz, 2 * fb))
        ring_sum(k)

    def turn(src, dst, begin, end):
        for i in range(begin, end, db // 8):
            dst[:, i:i + db // 8] = src[i:i + db // 8, :].T

    project(0)
    project(1)
    turn(r["wgu"], r["wgt"], 0, db // 2)
    ring_relay("0")

    arrive("sty_")
    stats = add_up(r["st1"][...], r["sty"], ny - 1)
    group_count = stats[1:2]
    group_mean = stats[0:1] / jnp.maximum(group_count, 1.0)
    all_count = jnp.sum(group_count, axis=1, keepdims=True)
    scale_of = TOKENS / jnp.maximum(all_count, 1.0)
    advantage, token_scale = [], []
    for t in range(4):
        mean_t = jnp.sum(jnp.where(lane == ids[t], group_mean, 0.0), axis=1, keepdims=True)
        advantage.append(reward[t] - mean_t)
        token_scale.append(mask[t] * scale_of)
    loads[11].wait()
    ring_relay("1")
    turn(r["wgu"], r["wgt"], db // 2, db)

    def hidden(h):
        k = str(h)
        total = ring_total(k)
        factors = total[:, 2 * fb:].astype(BF16)
        adapt = ADAPTER_SCALE * mm(factors, r["bd"][...])
        gate_base = total[:, :fb]
        up_base = total[:, fb:2 * fb]
        gate = gate_base + adapt[:, :fb]
        up = up_base + adapt[:, fb:]
        sig = jax.nn.sigmoid(gate)
        silu = gate * sig
        slope = sig * (1.0 + gate * (1.0 - sig))
        full = silu * up
        hp = full.astype(BF16)
        hd = (full - gate_base * jax.nn.sigmoid(gate_base) * up_base).astype(BF16)
        fd = ADAPTER_SCALE * mm_nt(hp, r["adown"][...])
        none = jnp.zeros_like(fd)
        fd = jnp.concatenate([none, fd] if h else [fd, none], axis=1)
        r["Hg" + k][z, :, :fb] = hd
        r["Hg" + k][z, :, fb:] = fd.astype(BF16)
        narrow_hand("H", k)
        r["Kg" + k][z, :, :fb] = (up * slope).astype(BF16)
        r["Kg" + k][z, :, fb:2 * fb] = silu.astype(BF16)
        r["Kg" + k][z, :, 2 * fb:] = factors
        r["hp" + k][...] = hp

    hidden(0)
    hidden(1)
    for i in range(8, 11):
        loads[i].wait()
    turn(r["downx"], r["dnt"], 0, fb + LANES)

    def outward(h):
        k = str(h)
        arrive("Hag" + k)
        both = r["Hg" + k][...].reshape(th, fb + LANES)
        pack(mm(both, r["downx"][...]).astype(BF16), "C", k)
        scatter_c("C", k)
        return both[:, fb:].astype(F32)

    row16 = lax.broadcasted_iota(jnp.int32, (16, 1), 0)
    even = (row16 & 1) == 0
    div = []

    def gradient(h):
        k = str(h)
        od = scatter_end("C", k)
        adv = jnp.where(even, advantage[2 * h], advantage[2 * h + 1])
        scl = jnp.where(even, token_scale[2 * h], token_scale[2 * h + 1])
        grad = scl * (KL_WEIGHT * od - adv * r["c32"][h])
        r["Dg" + k][y, x, c] = grad.astype(BF16)
        gather_y("D", k)
        square = od * od
        for t in range(2):
            picked = jnp.where(((row16 & 1) == t), square, 0.0)
            div.append(jnp.sum(jnp.sum(picked, axis=1, keepdims=True), axis=0, keepdims=True))

    fd0 = outward(0)
    scatter_x("C", "0")
    fd1 = outward(1)
    settle(20)
    narrow_hand("K", "0")
    r["fdp"][...] = (fd0 + fd1).astype(BF16).reshape(ne, th // ne, LANES)
    small_row("fd")
    scatter_y("C", "0")
    scatter_x("C", "1")
    gradient(0)
    narrow_hand("K", "1")
    scatter_y("C", "1")
    small_y("fd")
    gather_x("D", "0")
    gradient(1)
    dv = jnp.zeros((8, LANES), F32)
    for t in range(4):
        dv += jnp.where(row8 == t, div[t], 0.0)
    r["dv"][...] = dv * (0.5 / D)
    for i, device in enumerate(dev_z):
        send("dv_", i, r["dv"], r["dvr"].at[i], device)
    gather_c("D", "0")
    gather_x("D", "1")
    small_hand("fd")
    settle(20)

    def inward(h):
        k = str(h)
        arrive("Dc" + k)
        unpack("D", k, r["go" + k], 0)
        both = mm(r["go" + k][...], r["dnt"][...])
        gf = ADAPTER_SCALE * both[:, fb:]
        gh = both[:, :fb] + mm(gf[:, :RANK].astype(BF16), r["adown"][...])
        r["Eb" + k][...] = gh.astype(BF16).reshape(nz, tz, fb)
        narrow_sum("E", k)
        return gf

    gf0 = inward(0)
    gather_c("D", "1")
    gf1 = inward(1)
    r["Gb"][...] = jnp.where(lane < RANK, gf0, gf1).astype(BF16).reshape(nz, tz, LANES)
    for i, device in enumerate(dev_z):
        send("Grs", i, r["Gb"].at[zs[i]], r["Gr"].at[i], device)
    def adapters(h):
        k = str(h)
        total = narrow_total("E", k).astype(BF16)
        r["Eg" + k][z] = total
        narrow_hand("E", k)
        gh = total.astype(F32)
        gate = (gh * r["Kg" + k][z, :, :fb].astype(F32)).astype(BF16)
        up = (gh * r["Kg" + k][z, :, fb:2 * fb].astype(F32)).astype(BF16)
        ad = mm_nt(gate, r["bd"][:, :fb]) + mm_nt(up, r["bd"][:, fb:])
        r["adp"][h] = (ADAPTER_SCALE * ad).astype(BF16)

    adapters(0)
    adapters(1)
    for i, device in enumerate(dev_e):
        send("ade", i, r["adp"], r["adre"].at[i], device)
    arrive("fdE")
    fdf = r["fdf"][...].reshape(th, LANES)
    r["dog"][...] = mm_tn(fdf, r["go0"][...])[:RANK] + mm_tn(fdf, r["go1"][...])[RANK:]
    store(r["dog"], dog_o)
    arrive("Grs")
    gff = add_up(r["Gb"][z], r["Gr"], nz - 1).astype(BF16)
    gad = mm_tn(gff, r["hp0"][...])[:RANK] + mm_tn(gff, r["hp1"][...])[RANK:]
    rb, cb = plan.rb, plan.cb
    for j in range(nz):
        r["Mb"][j] = gad[j // 2 * rb:(j // 2 + 1) * rb, j % 2 * cb:(j % 2 + 1) * cb].astype(BF16)
    for i, device in enumerate(dev_z):
        send("Mrs", i, r["Mb"].at[zs[i]], r["Mr"].at[i], device)
    arrive("Kag0")
    arrive("Kag1")
    settle(28)

    def back(h):
        k = str(h)
        arrive("Eag" + k)
        gh = r["Eg" + k][...].reshape(th, fb).astype(F32)
        kept = r["Kg" + k][...].reshape(th, 2 * fb + LANES)
        r["ggu" + k][:, :fb] = (gh * kept[:, :fb].astype(F32)).astype(BF16)
        r["ggu" + k][:, fb:] = (gh * kept[:, fb:2 * fb].astype(F32)).astype(BF16)
        ggu = r["ggu" + k][...]
        ad = (ADAPTER_SCALE * mm_nt(ggu, r["bd"][...])).astype(BF16)
        gx = mm(ggu, r["wgt"][...]) + mm(ad, r["agu"][...])
        pack(gx.astype(BF16), "F", k)
        scatter_c("F", k)

    back(0)
    arrive("ade")
    r["ads"][...] = add_up(r["adp"][...], r["adre"], ne - 1).astype(BF16)
    for i, device in enumerate(dev_y):
        send("ady", i, r["ads"], r["adry"].at[i], device)
    scatter_x("F", "0")
    back(1)
    scatter_y("F", "0")
    arrive("ady")
    r["adf"][:, z] = add_up(r["ads"][...], r["adry"], ny - 1).astype(BF16)
    for i, device in enumerate(dev_z):
        send("adz", i, r["adf"].at[:, z], r["adf"].at[:, z], device)
    scatter_x("F", "1")
    settle(20)
    gu = jnp.zeros((LANES, 2 * fb), F32)
    for h in range(2):
        k = str(h)
        factors = r["Kg" + k][:, :, 2 * fb:].reshape(th, LANES)
        gu += mm_tn(factors, r["ggu" + k][...])
    r["gu"][...] = ADAPTER_SCALE * gu
    store(r["gu"].at[:RANK, :fb], gog_o)
    store(r["gu"].at[RANK:, fb:], uog_o)

    def input_gradient(h):
        gx = scatter_end("F", str(h))
        for q in range(NQ):
            r["o32"][2 * h:2 * h + 2, LANES * q:LANES * (q + 1)] = gx[2 * q:2 * q + 2]

    arrive("Mrs")
    r["Mg"][z] = add_up(r["Mb"][z], r["Mr"], nz - 1)
    for i, device in enumerate(dev_z):
        send("Mag", i, r["Mg"].at[z], r["Mg"].at[z], device)
    scatter_y("F", "1")
    arrive("adz")
    r["gab"][...] = mm_tn(r["adf"][...].reshape(2 * th, LANES), r["x"][...])
    store(r["gab"].at[:RANK], ag_o)
    store(r["gab"].at[RANK:], au_o)
    input_gradient(0)
    arrive("Mag")
    for j in range(nz):
        r["gad"][j // 2 * rb:(j // 2 + 1) * rb, j % 2 * cb:(j % 2 + 1) * cb] = r["Mg"][j]
    store(r["gad"], gad_o)
    arrive("dv_")
    dv = add_up(r["dv"][...], r["dvr"], nz - 1)
    for t in range(4):
        dv_o[t] = jnp.max(dv[t:t + 1, :])
    input_gradient(1)
    r["gx"][...] = r["o32"][...].astype(BF16)
    store(r["gx"], gx_o)
    settle()
    for copy in stores:
        copy.wait()


def finish_kernel(*refs):
    srcs, dsts, held, sems = refs[:8], refs[8:16], refs[16:24], refs[24]
    ins = [pltpu.make_async_copy(srcs[i], held[i], sems.at[i]) for i in range(8)]
    outs = [pltpu.make_async_copy(held[i], dsts[i], sems.at[8 + i]) for i in range(8)]
    for copy in ins:
        copy.start()
    for i in range(8):
        ins[i].wait()
        outs[i].start()
    for copy in outs:
        copy.wait()


def shards(wide, narrow, tokens, cotangent, rewards, group_ids, token_mask, w_gate, w_up, down_w,
           a_gate, a_up, gate_of, up_of, a_down, down_of):
    db, fb = w_gate.shape
    plan = Plan(wide, narrow, db, fb)
    hbm = pl.BlockSpec(memory_space=pltpu.HBM)
    sm = pl.BlockSpec(memory_space=pltpu.SMEM)
    s = jax.ShapeDtypeStruct
    shapes = (
        s((4, db), BF16), s((4,), F32), s((RANK, db), F32), s((RANK, db), F32),
        s((RANK, fb), F32), s((RANK, fb), F32), s((RANK, fb), F32), s((RANK, db), F32),
    )
    mids = pl.pallas_call(
        functools.partial(step_kernel, plan),
        out_shape=shapes,
        in_specs=[hbm, hbm, sm, sm, sm] + [hbm] * 9,
        out_specs=(hbm, sm) + (hbm,) * 6,
        scratch_shapes=plan.shapes,
        compiler_params=pltpu.CompilerParams(
            collective_id=0, has_side_effects=True, vmem_limit_bytes=60 << 20),
        name="policy_step",
    )(tokens, cotangent, rewards, group_ids, token_mask, w_gate, w_up, down_w, a_gate.T, a_up.T,
      gate_of, up_of, a_down.T, down_of)
    outs = pl.pallas_call(
        finish_kernel,
        out_shape=shapes,
        in_specs=[hbm] * 8,
        out_specs=(hbm,) * 8,
        scratch_shapes=[pltpu.VMEM(v.shape, v.dtype) for v in shapes]
        + [pltpu.SemaphoreType.DMA((16,))],
        compiler_params=pltpu.CompilerParams(vmem_limit_bytes=60 << 20),
        name="finish",
    )(*mids)
    gx, dv, ag, au, gog, uog, gad, dog = outs
    return gx, dv, ag.T, au.T, gog, uog, gad.T, dog


def solution(mesh):
    return jax.shard_map(
        functools.partial(shards, mesh.shape["wide"], mesh.shape["narrow"]),
        mesh=mesh,
        in_specs=(
            P("wide", "narrow"),
            P("wide", "narrow"),
            P("wide"),
            P("wide"),
            P("wide"),
            P("narrow", "wide"),
            P("narrow", "wide"),
            P("wide", "narrow"),
            P("narrow", None),
            P("narrow", None),
            P(None, "wide"),
            P(None, "wide"),
            P("wide", None),
            P(None, "narrow"),
        ),
        out_specs=(
            P("wide", "narrow"),
            P("wide"),
            P("narrow", None),
            P("narrow", None),
            P(None, "wide"),
            P(None, "wide"),
            P("wide", None),
            P(None, "narrow"),
        ),
        check_vma=False,
    )
```
